128 devices in a mesh: leaf: 32 (over x_lo, y, z), blk: 4 (over x_hi, core).
Axes of the slice: x: 4 (x_hi: 2, x_lo: 2; x = x_hi * 2 + x_lo), y: 4, z: 4, core: 2. Of those that a mesh axis runs over, the one named last changes fastest.
Arguments:
- stiffness: bfloat16 [64, 2048, 2048], P('leaf', 'blk'), may hold values from -6 to 6
- modes: bfloat16 [64, 2048, 512], P('leaf', 'blk'), may hold values from -0.125 to 0.125
- basis: bfloat16 [16384, 2048], P('leaf', 'blk'), may hold values from -0.125 to 0.125
- eigen: float32 [64, 512], P('leaf'), may hold values from 20 to 200
- counts: int32 [64], P('leaf'), may hold values from 80 to 400
- ancestry: int32 [64], P('leaf'), may hold values from 0 to 7
Outputs:
- projection: bfloat16 [64, 512, 2048], P('leaf', None, 'blk')
- correction: float32 [16384, 2048], P('leaf', 'blk')
The draws below stay inside these ranges and needn't reach their ends.
All inputs are finite; a program needn't handle non-finite values.
Results may differ from the reference program's by a relative error of at most 0.018.
Values may be sent and summed in bfloat16 or wider, within the bound.
No kernel may reach another device: no remote copies, remote signals or barrier semaphores. Data moves between devices by JAX's collectives and lax.ppermute only.
A program may use at most 192 MiB of HBM per device.

```python
import math
import jax
import jax.numpy as jnp
import numpy as np
from jax import lax

W = 2048
MCAP = 512
Q = 2048
R = 2048
SUBS = 64
NSEP = 8


def place_ends(drawn, key, smallest, high):
    longest = drawn.shape.index(max(drawn.shape))
    spots = []
    for shift in (0, 1):
        where = [jax.random.randint(jax.random.fold_in(key, axis), (), 0, length) for axis, length in enumerate(drawn.shape)]
        where[longest] = (where[longest] + shift) % drawn.shape[longest]
        spots.append(tuple(where))
    return drawn.at[spots[0]].set(smallest).at[spots[1]].set(high)


def block_levels(rng, dims, pieces, smallest, top_value):
    loudness, own = 1.0, jax.random.fold_in(rng, 6)
    for position, shards_of in pieces:
        draws = jnp.exp(jax.random.uniform(jax.random.fold_in(own, position), (shards_of,), jnp.float32, smallest / len(pieces), top_value / len(pieces)))
        loudness = loudness * jnp.repeat(draws, dims[position] // shards_of).reshape([-1 if axis == position else 1 for axis in range(len(dims))])
    return loudness


def cumulative_ranks(amount, skew):
    weights = [(1 << 20) // math.isqrt(grade ** skew) + 1 for grade in range(1, amount + 1)]
    deviation = 1 + sum(weights) // (1 << 30)
    return np.cumsum(np.array([max(1, weight // deviation) for weight in weights]))


def skewed_ids(own_key, extent, count, skew):
    grid = cumulative_ranks(count, skew)
    lot = jax.random.randint(jax.random.fold_in(own_key, 1), extent, 0, int(grid[count - 1]))
    rank = jnp.searchsorted(jnp.asarray(grid, jnp.int32), lot, side="right")
    return jax.random.permutation(jax.random.fold_in(own_key, 2), count)[rank].astype(jnp.int32)


def bell_draw(key, shape, deviation, reach, shards=(), kind=jnp.bfloat16):
    level = block_levels(key, shape, shards, -0.22, 0.18) if shards else 1.0
    entries = jax.random.normal(key, shape, jnp.float32) * deviation * level
    return jnp.minimum(jnp.maximum(entries, -reach), reach).astype(kind)


def setup_inputs(seed: int = 0) -> dict:
    arg_keys = jax.random.split(jax.random.key(seed), 7)
    return {
        "stiffness": bell_draw(arg_keys[0], (SUBS, R, Q), 1.0, 6.0, ((0, 32), (1, 4))),
        "modes": bell_draw(arg_keys[1], (SUBS, R, MCAP), R ** -0.5, 0.125, ((0, 32), (1, 4))),
        "basis": bell_draw(arg_keys[2], (NSEP * Q, W), Q ** -0.5, 0.125, ((0, 32), (1, 4))),
        "eigen": jnp.clip(jnp.exp(math.log(200.0) - 2.3025851 * jax.random.uniform(arg_keys[3], (SUBS, MCAP), jnp.float32) ** block_levels(arg_keys[3], (SUBS, MCAP), ((0, 32),), -0.2, 0.2)), 20.0, 200.0),
        "counts": place_ends(jax.random.randint(arg_keys[4], (SUBS,), MCAP * 5 // 32, MCAP * 25 // 32 + 1), jax.random.fold_in(arg_keys[4], 1), MCAP * 5 // 32, (MCAP * 25 // 32 + 1) - 1).astype(jnp.int32),
        "ancestry": place_ends(skewed_ids(arg_keys[5], (SUBS,), NSEP, 2), jax.random.fold_in(arg_keys[5], 3), 0, NSEP - 1).astype(jnp.int32),
    }


def reference(stiffness, modes, basis, eigen, counts, ancestry):
    wcols = basis.shape[1]
    slots = jnp.arange(MCAP, dtype=jnp.int32)

    def one_sub(carry, items):
        stiff, shapes, lam, count, anc = items
        coupled = jnp.dot(shapes.T, stiff, preferred_element_type=jnp.float32)
        coupled = jnp.where((slots < count)[:, None], coupled, 0.0).astype(jnp.bfloat16)
        first = (anc * Q).astype(jnp.int32)
        block = lax.dynamic_slice_in_dim(basis, first, Q, 0)
        proj = jnp.dot(coupled, block, preferred_element_type=jnp.float32).astype(jnp.bfloat16)
        scaled = (coupled.astype(jnp.float32) / lam[:, None]).astype(jnp.bfloat16)
        term = jnp.dot(scaled.T, proj, preferred_element_type=jnp.float32)
        old = lax.dynamic_slice_in_dim(carry, first, Q, 0)
        carry = lax.dynamic_update_slice_in_dim(carry, old + term, first, 0)
        return carry, proj

    start = jnp.zeros((NSEP * Q, wcols), jnp.float32)
    correction, projection = lax.scan(one_sub, start, (stiffness, modes, eigen, counts, ancestry))
    return projection, correction
```

```python
import jax
import jax.numpy as jnp
import numpy as np
from jax import lax
from jax.experimental import pallas as pl
from jax.experimental.pallas import tpu as pltpu
from jax.sharding import PartitionSpec as P

AXES = ("leaf", "blk")
SHAPE = (2, 4, 4, 2, 2)
ROWS = 400
TILE = 512
BF = jnp.bfloat16
F32 = jnp.float32


def shift(value, xl=0, y=0, z=0, xh=0, c=0):
    pairs = []
    for spot in np.ndindex(*SHAPE):
        to = tuple((a + b) % n for a, b, n in zip(spot, (xl, y, z, xh, c), SHAPE))
        pairs.append((int(np.ravel_multi_index(spot, SHAPE)), int(np.ravel_multi_index(to, SHAPE))))
    return lax.ppermute(value, AXES, pairs)


def tdot(a, b):
    return lax.dot_general(a, b, (((0,), (0,)), ((), ())), preferred_element_type=F32)


def couple_kernel(info, modes, stiffness, out):
    value = tdot(modes[0], stiffness[0])[:ROWS]
    row = lax.broadcasted_iota(jnp.int32, value.shape, 0)
    out[0] = jnp.where(row < info[2], value, 0.0).astype(BF)


def couple(sub, z, count, modes, stiffness):
    return pl.pallas_call(
        couple_kernel,
        out_shape=jax.ShapeDtypeStruct((4, ROWS, TILE), BF),
        grid_spec=pltpu.PrefetchScalarGridSpec(
            num_scalar_prefetch=1,
            grid=(4,),
            in_specs=[
                pl.BlockSpec((1, 512, 512), lambda d, info: (info[0], 0, 0)),
                pl.BlockSpec((1, 512, TILE), lambda d, info: (info[0], 0, lax.rem(info[1] + d, 4))),
            ],
            out_specs=pl.BlockSpec((1, ROWS, TILE), lambda d, info: (d, 0, 0)),
        ),
        compiler_params=pltpu.CompilerParams(vmem_limit_bytes=24 << 20),
        cost_estimate=pl.CostEstimate(flops=2 * 512 * 512 * 2048, bytes_accessed=4 << 20, transcendentals=0),
        name="couple",
    )(jnp.stack([sub, z, count]), modes, stiffness)


def project_kernel(slots, own, other, basis, out):
    j = pl.program_id(0)

    @pl.when(j == 0)
    def _():
        out[0] = jnp.dot(own[...], basis[0], preferred_element_type=F32).astype(BF)

    @pl.when(j == 1)
    def _():
        out[0] = jnp.dot(other[...], basis[0], preferred_element_type=F32).astype(BF)


def project(slots, own, other, basis):
    return pl.pallas_call(
        project_kernel,
        out_shape=jax.ShapeDtypeStruct((2, ROWS, TILE), BF),
        grid_spec=pltpu.PrefetchScalarGridSpec(
            num_scalar_prefetch=1,
            grid=(2,),
            in_specs=[
                pl.BlockSpec((ROWS, TILE), lambda j, s: (0, 0)),
                pl.BlockSpec((ROWS, TILE), lambda j, s: (0, 0)),
                pl.BlockSpec((1, TILE, TILE), lambda j, s: (s[j], 0, 0)),
            ],
            out_specs=pl.BlockSpec((1, ROWS, TILE), lambda j, s: (j, 0, 0)),
        ),
        compiler_params=pltpu.CompilerParams(vmem_limit_bytes=16 << 20),
        cost_estimate=pl.CostEstimate(flops=4 * ROWS * 512 * 512, bytes_accessed=3 << 20, transcendentals=0),
        name="project",
    )(slots, own, other, basis)


def correct_kernel(slots, *refs):
    coupled, scaled, outs, total = refs[:8], refs[8:12], refs[12:20], refs[20]
    total[...] = jnp.zeros_like(total)
    for d in range(4):
        for j in range(2):
            spot = slots[2 * d + j]
            total[spot] += tdot(coupled[2 * d + j][...], scaled[d][j])
    for k in range(8):
        outs[k][...] = total[k].astype(outs[k].dtype)


def correct(slots, coupled, scaled):
    width = scaled[0].shape[2]
    vmem = pl.BlockSpec(memory_space=pltpu.VMEM)
    kinds = [F32] + [BF] * 7
    return pl.pallas_call(
        correct_kernel,
        out_shape=[jax.ShapeDtypeStruct((TILE, width), kind) for kind in kinds],
        in_specs=[pl.BlockSpec(memory_space=pltpu.SMEM)] + [vmem] * 12,
        out_specs=[vmem] * 8,
        scratch_shapes=[pltpu.VMEM((8, TILE, width), F32)],
        compiler_params=pltpu.CompilerParams(vmem_limit_bytes=40 << 20),
        cost_estimate=pl.CostEstimate(flops=16 * ROWS * 512 * width, bytes_accessed=8 << 20, transcendentals=0),
        name="correct",
    )(slots, *coupled, *scaled)


def per_device(stiffness, modes, basis, eigen, counts, ancestry):
    leaf, blk = lax.axis_index("leaf"), lax.axis_index("blk")
    xl, y, z = leaf // 16, (leaf // 4) % 4, leaf % 4
    c = blk % 2
    groups = [[g * 4 + k for g in range(8)] for k in range(4)]
    every = lax.all_gather(basis, "leaf", axis=0, tiled=False, axis_index_groups=groups)
    ancestors = lax.all_gather(ancestry, "leaf", axis=0, tiled=False)

    away = couple(1 - c, z, counts[1 - c], modes, stiffness)
    came = shift(away, c=1)
    kept = couple(c, z, counts[c], modes, stiffness)
    both = [(kept[d].astype(F32) + came[d].astype(F32)).astype(BF) for d in range(4)]
    half = [both[0]] + [shift(both[d], z=d) for d in range(1, 4)]
    own, other, slots, parts = [None] * 4, [None] * 4, [None] * 4, [None] * 4
    for d in (0, 1, 3, 2):
        met = shift(half[d], xh=1)
        own[d] = (half[d].astype(F32) + met.astype(F32)).astype(BF)
        other[d] = shift(own[d], c=1)
        theirs = ancestors[xl * 16 + y * 4 + (z - d) % 4]
        slots[d] = jnp.stack([theirs[c], theirs[1 - c]])
        parts[d] = project(slots[d], own[d], other[d], every)
    heard = [parts[0]] + [shift(parts[d], z=-d) for d in (1, 2, 3)]
    mine = sum(h.astype(F32) for h in heard)
    swap = c == 1
    ordered = jnp.where(swap, mine[::-1], mine).astype(BF)
    projection = jnp.pad(ordered, ((0, 0), (0, 512 - ROWS), (0, 0)))
    lam = jnp.where(swap, eigen[::-1], eigen)[:, :ROWS, None]
    scaled = (mine / lam).astype(BF)

    places = jnp.concatenate(slots)
    places = ((places // 4 - xl) % 2) * 4 + (places % 4 - y) % 4
    coupled = [item for d in range(4) for item in (own[d], other[d])]
    columns = []
    for h in range(2):
        piece = scaled[:, :, h * 256 : (h + 1) * 256]
        pieces = [piece] + [shift(piece, z=d) for d in (1, 2, 3)]
        terms = correct(places, coupled, pieces)
        total = terms[0]
        for k in range(1, 8):
            total = total + shift(terms[k], xl=k // 4, y=k % 4).astype(F32)
        columns.append(total)
    return projection, jnp.concatenate(columns, axis=1)


def solution(mesh):
    placed = (
        P("leaf", "blk", None),
        P("leaf", "blk", None),
        P("leaf", "blk"),
        P("leaf", None),
        P("leaf"),
        P("leaf"),
    )
    return jax.shard_map(
        per_device,
        mesh=mesh,
        in_specs=placed,
        out_specs=(P("leaf", None, "blk"), P("leaf", "blk")),
        check_vma=False,
    )
```

```python
import jax
import jax.numpy as jnp
import numpy as np
from jax import lax
from jax.experimental import pallas as pl
from jax.experimental.pallas import tpu as pltpu
from jax.sharding import PartitionSpec as P

AXES = ("leaf", "blk")
SHAPE = (2, 4, 4, 2, 2)
ROWS = 400
LINES = 416
TILE = 512
WIDTHS = (256, 256)
BF = jnp.bfloat16
F32 = jnp.float32
VMEM = pl.BlockSpec(memory_space=pltpu.VMEM)
SMEM = pl.BlockSpec(memory_space=pltpu.SMEM)


def shift(value, xl=0, y=0, z=0, xh=0, c=0):
    pairs = []
    for spot in np.ndindex(*SHAPE):
        to = tuple((a + b) % n for a, b, n in zip(spot, (xl, y, z, xh, c), SHAPE))
        pairs.append((int(np.ravel_multi_index(spot, SHAPE)), int(np.ravel_multi_index(to, SHAPE))))
    return lax.ppermute(value, AXES, pairs)


def tdot(a, b):
    return lax.dot_general(a, b, (((0,), (0,)), ((), ())), preferred_element_type=F32)


def couple(which, spot, counts, ancestry, modes, stiffness):
    def side(spot):
        return spot[3] if which == 0 else 1 - spot[3]

    def kernel(spot, counts, ancestry, modes, stiffness, out, turned):
        @pl.when(pl.program_id(0) == 0)
        def _():
            turned[...] = modes[0].astype(F32).T[:ROWS].astype(BF)

        value = jnp.dot(turned[...], stiffness[0], preferred_element_type=F32)
        row = lax.broadcasted_iota(jnp.int32, value.shape, 0)
        out[0, pl.ds(0, ROWS)] = jnp.where(row < counts[side(spot)], value, 0.0).astype(BF)
        tag = jnp.zeros((LINES - ROWS, TILE), F32)
        if which == 0:
            row = lax.broadcasted_iota(jnp.int32, tag.shape, 0)
            for j in range(2):
                tag = jnp.where(row == j, ancestry[spot[3] ^ j].astype(F32), tag)
        out[0, pl.ds(ROWS, LINES - ROWS)] = tag.astype(BF)

    return pl.pallas_call(
        kernel,
        out_shape=jax.ShapeDtypeStruct((4, LINES, TILE), BF),
        grid_spec=pltpu.PrefetchScalarGridSpec(
            num_scalar_prefetch=3,
            grid=(4,),
            in_specs=[
                pl.BlockSpec((1, 512, 512), lambda d, spot, *_: (side(spot), 0, 0)),
                pl.BlockSpec((1, 512, TILE), lambda d, spot, *_: (side(spot), 0, (spot[2] + d) & 3)),
            ],
            out_specs=pl.BlockSpec((1, LINES, TILE), lambda d, *_: (d, 0, 0)),
            scratch_shapes=[pltpu.VMEM((ROWS, 512), BF)],
        ),
        compiler_params=pltpu.CompilerParams(vmem_limit_bytes=56 << 20),
        cost_estimate=pl.CostEstimate(flops=2 * 512 * 512 * 2048, bytes_accessed=4 << 20, transcendentals=0),
        name="couple",
    )(spot, counts, ancestry, modes, stiffness)


def relative(separator, spot):
    return ((separator >> 2) ^ spot[0]) * 4 + ((separator - spot[1]) & 3)


def ancestor(own, j):
    tag = own[pl.ds(ROWS, LINES - ROWS), pl.ds(0, 128)].astype(F32)
    row = lax.broadcasted_iota(jnp.int32, tag.shape, 0)
    return jnp.max(jnp.where(row == j, tag * 0.5, 0.0)).astype(jnp.int32)


def project(spot, own, other, tiles):
    def kernel(spot, own, other, *refs):
        tiles, out, held = refs[:8], refs[8], refs[9]
        for j, side in enumerate((own, other)):
            place = relative(ancestor(own, j), spot)
            for k in range(8):

                @pl.when(place == k)
                def _():
                    held[...] = tiles[k][...]

            out[j] = jnp.dot(side[pl.ds(0, ROWS)], held[...], preferred_element_type=F32).astype(BF)

    return pl.pallas_call(
        kernel,
        out_shape=jax.ShapeDtypeStruct((2, ROWS, TILE), BF),
        in_specs=[SMEM] + [VMEM] * 10,
        out_specs=VMEM,
        scratch_shapes=[pltpu.VMEM((TILE, TILE), BF)],
        compiler_params=pltpu.CompilerParams(vmem_limit_bytes=16 << 20),
        cost_estimate=pl.CostEstimate(flops=4 * ROWS * 512 * 512, bytes_accessed=3 << 20, transcendentals=0),
        name="project",
    )(spot, own, other, *tiles)


def finish(spot, eigen, parts):
    def kernel(spot, eigen, *refs):
        parts, projection, outs = refs[:4], refs[4], refs[5:]
        for j in range(2):
            side = spot[3] ^ j
            value = sum(part[j].astype(F32) for part in parts)
            projection[side, pl.ds(0, ROWS)] = value.astype(BF)
            projection[side, pl.ds(ROWS, 512 - ROWS)] = jnp.zeros((512 - ROWS, TILE), BF)
            scaled = (value / eigen[side, pl.ds(0, ROWS)]).astype(BF)
            first = 0
            for out, width in zip(outs, WIDTHS):
                out[j] = scaled[:, first : first + width]
                first += width

    return pl.pallas_call(
        kernel,
        out_shape=[jax.ShapeDtypeStruct((2, 512, TILE), BF)]
        + [jax.ShapeDtypeStruct((2, ROWS, width), BF) for width in WIDTHS],
        in_specs=[SMEM] + [VMEM] * 5,
        out_specs=[VMEM] * (1 + len(WIDTHS)),
        compiler_params=pltpu.CompilerParams(vmem_limit_bytes=24 << 20),
        cost_estimate=pl.CostEstimate(flops=8 * ROWS * 512, bytes_accessed=5 << 20, transcendentals=0),
        name="finish",
    )(spot, eigen, *parts)


def correct(spot, coupled, scaled):
    width = scaled[0].shape[2]

    def kernel(spot, *refs):
        coupled, scaled, outs, total = refs[:8], refs[8:12], refs[12:16], refs[16]
        total[...] = jnp.zeros_like(total)
        for d in range(4):
            for j in range(2):
                place = relative(ancestor(coupled[2 * d], j), spot)
                total[place] += tdot(coupled[2 * d + j][pl.ds(0, ROWS)], scaled[d][j])
        for k in range(8):
            outs[k % 4][k // 4] = total[k].astype(BF)

    return pl.pallas_call(
        kernel,
        out_shape=[jax.ShapeDtypeStruct((2, TILE, width), BF)] * 4,
        in_specs=[SMEM] + [VMEM] * 12,
        out_specs=[VMEM] * 4,
        scratch_shapes=[pltpu.VMEM((8, TILE, width), F32)],
        compiler_params=pltpu.CompilerParams(vmem_limit_bytes=32 << 20),
        cost_estimate=pl.CostEstimate(flops=16 * ROWS * 512 * width, bytes_accessed=8 << 20, transcendentals=0),
        name="correct",
    )(spot, *coupled, *scaled)


def per_device(stiffness, modes, basis, eigen, counts, ancestry):
    leaf, blk = lax.axis_index("leaf"), lax.axis_index("blk")
    spot = jnp.stack([leaf >> 4, (leaf >> 2) & 3, leaf & 3, blk & 1])

    away = couple(1, spot, counts, ancestry, modes, stiffness)
    came = shift(away, c=1)
    crossed = shift(basis, xl=1)
    above, below = shift(basis, y=-1), shift(basis, y=1)
    kept = couple(0, spot, counts, ancestry, modes, stiffness)
    both = [(kept[d].astype(F32) + came[d].astype(F32)).astype(BF) for d in range(4)]
    half = {d: shift(both[d], z=d) if d else both[0] for d in (0, 2, 1, 3)}
    own, other, parts = {}, {}, {}

    def meet(d, extra):
        met = shift(half[d], xh=1)
        met, *extra = lax.optimization_barrier((met, *extra))
        own[d] = (half[d].astype(F32) + met.astype(F32)).astype(BF)
        other[d] = shift(own[d], c=1)
        return extra

    crossed, above, below = meet(0, (crossed, above, below))
    cabove, cbelow = shift(crossed, y=-1), shift(crossed, y=1)
    cabove, cbelow = meet(2, (cabove, cbelow))
    mid = TILE // 2
    far1 = shift(jnp.stack([above[:mid], cabove[:mid]]), y=-1)
    far2 = shift(jnp.stack([below[mid:], cbelow[mid:]]), y=1)
    far1, far2 = meet(1, (far1, far2))
    meet(3, ())
    far = jnp.concatenate([far1, far2], axis=1)
    tiles = [basis, above, far[0], below, crossed, cabove, far[1], cbelow]
    for d in (0, 2, 1, 3):
        part = project(spot, own[d], other[d], tiles)
        parts[d] = shift(part, z=-d) if d else part
    lam = eigen[:, :, None]
    projection, *scaled = finish(spot, lam, [parts[d] for d in range(4)])

    coupled = [item for d in range(4) for item in (own[d], other[d])]
    columns = []
    for piece in scaled:
        pieces = [piece] + [shift(piece, z=d) for d in (1, 2, 3)]
        terms = correct(spot, coupled, pieces)
        total = terms[0].astype(F32) + sum(shift(terms[k], y=k).astype(F32) for k in (2, 1, 3))
        columns.append(total[0] + shift(total[1].astype(BF), xl=1).astype(F32))
    return projection, jnp.concatenate(columns, axis=1)


def solution(mesh):
    placed = (
        P("leaf", "blk", None),
        P("leaf", "blk", None),
        P("leaf", "blk"),
        P("leaf", None),
        P("leaf"),
        P("leaf"),
    )
    return jax.shard_map(
        per_device,
        mesh=mesh,
        in_specs=placed,
        out_specs=(P("leaf", None, "blk"), P("leaf", "blk")),
        check_vma=False,
    )
```

```python
import jax
import jax.numpy as jnp
import numpy as np
from jax import lax
from jax.experimental import pallas as pl
from jax.experimental.pallas import tpu as pltpu
from jax.sharding import PartitionSpec as P

AXES = ("leaf", "blk")
SHAPE = (2, 4, 4, 2, 2)
ROWS = 400
LINES = 416
TILE = 512
WIDTHS = (256, 256)
ORDER = (2, 1, 3, 0)
BF = jnp.bfloat16
F32 = jnp.float32
VMEM = pl.BlockSpec(memory_space=pltpu.VMEM)
SMEM = pl.BlockSpec(memory_space=pltpu.SMEM)
HBM = pl.BlockSpec(memory_space=pltpu.HBM)
ANY = pl.BlockSpec(memory_space=pl.ANY)


def shift(value, xl=0, y=0, z=0, xh=0, c=0):
    pairs = []
    for spot in np.ndindex(*SHAPE):
        to = tuple((a + b) % n for a, b, n in zip(spot, (xl, y, z, xh, c), SHAPE))
        pairs.append((int(np.ravel_multi_index(spot, SHAPE)), int(np.ravel_multi_index(to, SHAPE))))
    return lax.ppermute(value, AXES, pairs)


def tdot(a, b):
    return lax.dot_general(a, b, (((0,), (0,)), ((), ())), preferred_element_type=F32)


def couple(which, spot, modes, stiffness):
    def kernel(spot, modes, stiffness, out):
        sub = spot[3] ^ which
        tag = jnp.zeros((LINES - ROWS, TILE), F32)
        if which == 0:
            places = [relative(spot[6 + (spot[3] ^ j)], spot) for j in range(2)]
            tag = tag + (places[0] + 8 * places[1]).astype(F32)
        live = lax.broadcasted_iota(jnp.int32, (ROWS, TILE), 0) < spot[4 + sub]
        turned = modes[sub].astype(F32).T[:ROWS].astype(BF)
        for k, d in enumerate(ORDER):
            first = pl.multiple_of(((spot[2] + d) & 3) * TILE, TILE)
            value = jnp.dot(turned, stiffness[sub, :, pl.ds(first, TILE)], preferred_element_type=F32)
            out[k, pl.ds(0, ROWS)] = jnp.where(live, value, 0.0).astype(BF)
            out[k, pl.ds(ROWS, LINES - ROWS)] = tag.astype(BF)

    return pl.pallas_call(
        kernel,
        out_shape=jax.ShapeDtypeStruct((4, LINES, TILE), BF),
        in_specs=[SMEM] + [VMEM] * 2,
        out_specs=VMEM,
        compiler_params=pltpu.CompilerParams(vmem_limit_bytes=20 << 20),
        cost_estimate=pl.CostEstimate(flops=2 * 512 * 512 * 2048, bytes_accessed=4 << 20, transcendentals=0),
        name="couple",
    )(spot, modes, stiffness)


def relative(separator, spot):
    return ((separator >> 2) ^ spot[0]) * 4 + ((separator - spot[1]) & 3)


def places_of(own):
    tag = own[pl.ds(ROWS, 8), pl.ds(0, 128)].astype(F32)
    both = (jnp.max(tag) * 0.5).astype(jnp.int32)
    return both & 7, both >> 3


def project(own, other, tiles):
    def kernel(own, other, *refs):
        tiles, out, held, sems = refs[:8], refs[8], refs[9], refs[10]
        for j, place in enumerate(places_of(own)):
            for k in range(8):

                @pl.when(place == k)
                def _():
                    pltpu.make_async_copy(tiles[k], held.at[j], sems.at[j]).start()

        for j, side in enumerate((own, other)):
            pltpu.make_async_copy(tiles[0], held.at[j], sems.at[j]).wait()
            out[j] = jnp.dot(side[pl.ds(0, ROWS)], held[j], preferred_element_type=F32).astype(BF)

    return pl.pallas_call(
        kernel,
        out_shape=jax.ShapeDtypeStruct((2, ROWS, TILE), BF),
        in_specs=[VMEM] * 2 + [ANY] * 8,
        out_specs=VMEM,
        scratch_shapes=[pltpu.VMEM((2, TILE, TILE), BF), pltpu.SemaphoreType.DMA((2,))],
        compiler_params=pltpu.CompilerParams(vmem_limit_bytes=8 << 20),
        cost_estimate=pl.CostEstimate(flops=4 * ROWS * 512 * 512, bytes_accessed=3 << 20, transcendentals=0),
        name="project",
    )(own, other, *tiles)


def scale(eigen, parts):
    def kernel(eigen, *refs):
        parts, outs = refs[:4], refs[4:]
        for j in range(2):
            value = sum(part[j].astype(F32) for part in parts)
            scaled = (value * (1.0 / eigen[j, pl.ds(0, ROWS)])).astype(BF)
            first = 0
            for out, width in zip(outs, WIDTHS):
                out[j] = scaled[:, first : first + width]
                first += width

    return pl.pallas_call(
        kernel,
        out_shape=[jax.ShapeDtypeStruct((2, ROWS, width), BF) for width in WIDTHS],
        in_specs=[VMEM] * 5,
        out_specs=[VMEM] * len(WIDTHS),
        compiler_params=pltpu.CompilerParams(vmem_limit_bytes=14 << 20),
        cost_estimate=pl.CostEstimate(flops=8 * ROWS * 512, bytes_accessed=5 << 20, transcendentals=0),
        name="scale",
    )(eigen, *parts)


def correct(coupled, scaled):
    width = scaled[0].shape[2]

    def kernel(*refs):
        coupled, scaled, outs, total = refs[:8], refs[8:-5], refs[-5:-1], refs[-1]
        scaled = [ref.at[j] for ref in scaled for j in range(ref.shape[0])]
        total[...] = jnp.zeros_like(total)
        for d in range(4):
            for j, place in enumerate(places_of(coupled[2 * d])):
                total[place] += tdot(coupled[2 * d + j][pl.ds(0, ROWS)], scaled[2 * d + j][...])
        for k in range(8):
            outs[k % 4][k // 4] = total[k].astype(BF)

    return pl.pallas_call(
        kernel,
        out_shape=[jax.ShapeDtypeStruct((2, TILE, width), BF)] * 4,
        in_specs=[VMEM] * (8 + len(scaled)),
        out_specs=[VMEM] * 4,
        scratch_shapes=[pltpu.VMEM((8, TILE, width), F32)],
        compiler_params=pltpu.CompilerParams(vmem_limit_bytes=20 << 20),
        cost_estimate=pl.CostEstimate(flops=16 * ROWS * 512 * width, bytes_accessed=8 << 20, transcendentals=0),
        name="correct",
    )(*coupled, *scaled)


def add(a, b):
    return (a.astype(F32) + b.astype(F32)).astype(BF)


def per_device(stiffness, modes, basis, eigen, counts, ancestry):
    leaf, blk = lax.axis_index("leaf"), lax.axis_index("blk")
    spot = jnp.stack([leaf >> 4, (leaf >> 2) & 3, leaf & 3, blk & 1, counts[0], counts[1], ancestry[0], ancestry[1]])

    crossed = shift(basis, xl=1)
    above, below = shift(basis, y=-1), shift(basis, y=1)
    away = couple(1, spot, modes, stiffness)
    came = shift(away, c=1)
    kept = couple(0, spot, modes, stiffness)
    cabove, cbelow = shift(crossed, y=-1), shift(crossed, y=1)

    both = add(kept, came)
    met2, met13, met0 = (shift(both[k], xh=1) for k in (slice(0, 1), slice(1, 3), slice(3, 4)))
    met2, above, below, cabove, cbelow = lax.optimization_barrier((met2, above, below, cabove, cbelow))
    mid = TILE // 2
    far1 = shift(jnp.stack([above[:mid], cabove[:mid]]), y=-1)
    far2 = shift(jnp.stack([below[mid:], cbelow[mid:]]), y=1)
    own, other, parts = {}, {}, {}
    own[2] = shift(add(both[0], met2[0]), z=2)
    met13, far1, far2, own[2] = lax.optimization_barrier((met13, far1, far2, own[2]))
    other[2] = shift(own[2], c=1)
    own[1] = shift(add(both[1], met13[0]), z=1)
    own[3] = shift(add(both[2], met13[1]), z=3)
    far = jnp.concatenate([far1, far2], axis=1)
    tiles = [basis, above, far[0], below, crossed, cabove, far[1], cbelow]
    part = project(own[2], other[2], tiles)
    parts[2] = shift(part, z=2)
    own[1], own[3], met0, part = lax.optimization_barrier((own[1], own[3], met0, part))
    own[0] = add(both[3], met0[0])
    for d in (1, 3, 0):
        other[d] = shift(own[d], c=1)
        part = project(own[d], other[d], tiles)
        parts[d] = shift(part, z=-d) if d else part
    parts = [parts[d] for d in range(4)]
    swap = (blk & 1) == 1
    lam = jnp.where(swap, eigen[::-1], eigen)[:, :, None]
    scaled = scale(lam, parts)

    coupled = [item for d in range(4) for item in (own[d], other[d])]
    columns = []
    for h, piece in enumerate(scaled):
        if h == 0:
            pieces = [piece] + [shift(piece, z=d) for d in (1, 2, 3)]
        else:
            up, down = shift(piece, z=1), shift(piece, z=-1)
            pieces = [piece, up, shift(up[:1], z=1), shift(down[1:], z=-1), down]
        terms = correct(coupled, pieces)
        total = terms[0].astype(F32) + sum(shift(terms[k], y=k).astype(F32) for k in (2, 1, 3))
        columns.append(total[0] + shift(total[1].astype(BF), xl=1).astype(F32))
    mine = sum(part.astype(F32) for part in parts)
    mine = jnp.where(swap, mine[::-1], mine).astype(BF)
    projection = jnp.pad(mine, ((0, 0), (0, 512 - ROWS), (0, 0)))
    return projection, jnp.concatenate(columns, axis=1)


def solution(mesh):
    placed = (
        P("leaf", "blk", None),
        P("leaf", "blk", None),
        P("leaf", "blk"),
        P("leaf", None),
        P("leaf"),
        P("leaf"),
    )
    return jax.shard_map(
        per_device,
        mesh=mesh,
        in_specs=placed,
        out_specs=(P("leaf", None, "blk"), P("leaf", "blk")),
        check_vma=False,
    )
```

```python
import jax
import jax.numpy as jnp
import numpy as np
from jax import lax
from jax.experimental import pallas as pl
from jax.experimental.pallas import tpu as pltpu
from jax.sharding import PartitionSpec as P

AXES = ("leaf", "blk")
SHAPE = (2, 4, 4, 2, 2)
ROWS = 400
LINES = 416
SPARE = 416
TILE = 512
WIDTHS = (256, 256)
ORDER = (2, 1, 3, 0)
BF = jnp.bfloat16
F32 = jnp.float32
VMEM = pl.BlockSpec(memory_space=pltpu.VMEM)
SMEM = pl.BlockSpec(memory_space=pltpu.SMEM)
HBM = pl.BlockSpec(memory_space=pltpu.HBM)
ANY = pl.BlockSpec(memory_space=pl.ANY)


def shift(value, xl=0, y=0, z=0, xh=0, c=0):
    pairs = []
    for spot in np.ndindex(*SHAPE):
        to = tuple((a + b) % n for a, b, n in zip(spot, (xl, y, z, xh, c), SHAPE))
        pairs.append((int(np.ravel_multi_index(spot, SHAPE)), int(np.ravel_multi_index(to, SHAPE))))
    return lax.ppermute(value, AXES, pairs)


def tdot(a, b):
    return lax.dot_general(a, b, (((0,), (0,)), ((), ())), preferred_element_type=F32)


def couple(which, spot, modes, stiffness):
    def kernel(spot, modes, stiffness, *outs):
        sub = spot[3] ^ which
        tag = jnp.zeros((LINES - ROWS, TILE), F32)
        if which == 0:
            places = [relative(spot[6 + (spot[3] ^ j)], spot) for j in range(2)]
            tag = tag + (places[0] + 8 * places[1]).astype(F32)
        live = lax.broadcasted_iota(jnp.int32, (ROWS, TILE), 0) < spot[4 + sub]
        turned = modes[sub].astype(F32).T[:ROWS].astype(BF)
        for k, d in enumerate(ORDER):
            first = pl.multiple_of(((spot[2] + d) & 3) * TILE, TILE)
            value = jnp.dot(turned, stiffness[sub, :, pl.ds(first, TILE)], preferred_element_type=F32)
            outs[k][0, pl.ds(0, ROWS)] = jnp.where(live, value, 0.0).astype(BF)
            outs[k][0, pl.ds(ROWS, LINES - ROWS)] = tag.astype(BF)

    return pl.pallas_call(
        kernel,
        out_shape=[jax.ShapeDtypeStruct((1, LINES, TILE), BF)] * 4,
        in_specs=[SMEM] + [VMEM] * 2,
        out_specs=[VMEM] * 4,
        compiler_params=pltpu.CompilerParams(vmem_limit_bytes=20 << 20),
        cost_estimate=pl.CostEstimate(flops=1 << 10, bytes_accessed=1 << 10, transcendentals=0),
        name="couple",
    )(spot, modes, stiffness)


def relative(separator, spot):
    return ((separator >> 2) ^ spot[0]) * 4 + ((separator - spot[1]) & 3)


def tag_of(own):
    return own[pl.ds(ROWS, 8), pl.ds(0, 128)].astype(F32)


def places_of(own):
    both = (jnp.max(tag_of(own)) * 0.5).astype(jnp.int32)
    return both & 7, both >> 3


def halves(value):
    first, out = 0, []
    for width in WIDTHS:
        out.append(value[..., first : first + width])
        first += width
    return out


def project(sides, tiles, carry=(), whole=False):
    count = len(sides)
    slots = [slot for slot, _ in carry]

    def kernel(*refs):
        sides, tiles = refs[: 2 * count], refs[2 * count : 2 * count + 8]
        carried = refs[2 * count + 8 : 2 * count + 8 + len(slots)]
        outs, (held, sems) = refs[2 * count + 8 + len(slots) : -2], refs[-2:]
        for n in range(count):
            for j, place in enumerate(places_of(sides[2 * n])):
                for k in range(8):

                    @pl.when(place == k)
                    def _():
                        pltpu.make_async_copy(tiles[k], held.at[2 * n + j], sems.at[2 * n + j]).start()

        for n in range(2 * count):
            pltpu.make_async_copy(tiles[0], held.at[n], sems.at[n]).wait()
            value = jnp.dot(sides[n][pl.ds(0, ROWS)], held[n], preferred_element_type=F32)
            if slots and slots[n // 2] == n % 2:
                value = value + carried[n // 2][0, pl.ds(0, ROWS)].astype(F32)
            if whole:
                outs[n][0, pl.ds(0, ROWS)] = value.astype(BF)
                outs[n][0, pl.ds(ROWS, SPARE - ROWS)] = jnp.zeros((SPARE - ROWS, TILE), BF)
                continue
            for h, half in enumerate(halves(value)):
                outs[n // 2 * len(WIDTHS) + h][n % 2] = half.astype(BF)

    shapes = [(1, SPARE, TILE)] * 2 if whole else [(2, ROWS, width) for width in WIDTHS] * count
    flat = pl.pallas_call(
        kernel,
        out_shape=[jax.ShapeDtypeStruct(shape, BF) for shape in shapes],
        in_specs=[VMEM] * (2 * count) + [ANY] * 8 + [VMEM] * len(slots),
        out_specs=[VMEM] * len(shapes),
        scratch_shapes=[pltpu.VMEM((2 * count, TILE, TILE), BF), pltpu.SemaphoreType.DMA((2 * count,))],
        compiler_params=pltpu.CompilerParams(vmem_limit_bytes=12 << 20),
        cost_estimate=pl.CostEstimate(flops=1 << 10, bytes_accessed=1 << 10, transcendentals=0),
        name="project",
    )(*[item for pair in sides for item in pair], *tiles, *[item for _, item in carry])
    if whole:
        return flat
    return [flat[n * len(WIDTHS) : (n + 1) * len(WIDTHS)] for n in range(count)]


def scale(eigen, parts):
    def kernel(eigen, first, second, third, total, scaled):
        for j in range(2):
            value = first[j].astype(F32) + second[j].astype(F32) + third[j].astype(F32)
            total[j] = value.astype(BF)
            scaled[j] = (value * (1.0 / eigen[j, pl.ds(0, ROWS)])).astype(BF)

    return pl.pallas_call(
        kernel,
        out_shape=[jax.ShapeDtypeStruct(parts[0].shape, BF)] * 2,
        in_specs=[VMEM] * 4,
        out_specs=[VMEM] * 2,
        compiler_params=pltpu.CompilerParams(vmem_limit_bytes=10 << 20),
        cost_estimate=pl.CostEstimate(flops=1 << 10, bytes_accessed=1 << 10, transcendentals=0),
        name="scale",
    )(eigen, *parts)


def correct(coupled, scaled):
    width = scaled[0].shape[2]

    def kernel(*refs):
        coupled, scaled, outs, total = refs[:8], refs[8:-5], refs[-5:-1], refs[-1]
        scaled = [ref.at[j] for ref in scaled for j in range(ref.shape[0])]
        total[...] = jnp.zeros_like(total)
        tags = sum(tag_of(coupled[2 * d]) * (0.5 * 64**d) for d in range(4))
        places = jnp.max(tags).astype(jnp.int32)
        for d in range(4):
            for j in range(2):
                place = (places >> (6 * d + 3 * j)) & 7
                total[place] += tdot(coupled[2 * d + j][pl.ds(0, ROWS)], scaled[2 * d + j][...])
        for k in range(8):
            outs[k % 4][k // 4] = total[k].astype(BF)

    return pl.pallas_call(
        kernel,
        out_shape=[jax.ShapeDtypeStruct((2, TILE, width), BF)] * 4,
        in_specs=[VMEM] * (8 + len(scaled)),
        out_specs=[VMEM] * 4,
        scratch_shapes=[pltpu.VMEM((8, TILE, width), F32)],
        compiler_params=pltpu.CompilerParams(vmem_limit_bytes=20 << 20),
        cost_estimate=pl.CostEstimate(flops=1 << 10, bytes_accessed=1 << 10, transcendentals=0),
        name="correct",
    )(*coupled, *scaled)


def add(a, b):
    return (a.astype(F32) + b.astype(F32)).astype(BF)


def per_device(stiffness, modes, basis, eigen, counts, ancestry):
    leaf, blk = lax.axis_index("leaf"), lax.axis_index("blk")
    spot = jnp.stack([leaf >> 4, (leaf >> 2) & 3, leaf & 3, blk & 1, counts[0], counts[1], ancestry[0], ancestry[1]])

    crossed = shift(basis, xl=1)
    above, below = shift(basis, y=-1), shift(basis, y=1)
    away = couple(1, spot, modes, stiffness)
    came = [shift(piece, c=1) for piece in away]
    kept = couple(0, spot, modes, stiffness)
    both = [add(*pair) for pair in zip(kept, came)]
    crossed, *_ = lax.optimization_barrier((crossed, *both))
    cabove, cbelow = shift(crossed, y=-1), shift(crossed, y=1)
    met2, met13, met0 = (shift(item, xh=1) for item in (both[0], jnp.concatenate(both[1:3]), both[3]))
    met2, above, below = lax.optimization_barrier((met2, above, below))
    own, other = {}, {}
    own[2] = shift(add(both[0][0], met2[0]), z=2)
    mid = TILE // 2
    far1 = shift(jnp.stack([above[:mid], cabove[:mid]]), y=-1)
    far2 = shift(jnp.stack([below[mid:], cbelow[mid:]]), y=1)
    other[2] = shift(own[2][:ROWS], c=1)
    met13, other[2], far1, far2 = lax.optimization_barrier((met13, other[2], far1, far2))
    own[1] = shift(add(both[1][0], met13[0]), z=1)
    own[3] = shift(add(both[2][0], met13[1]), z=3)
    far = jnp.concatenate([far1, far2], axis=1)
    tiles = [basis, above, far[0], below, crossed, cabove, far[1], cbelow]
    part = project([(own[2], other[2])], tiles, whole=True)
    carry1, carry3 = shift(part[0], z=-1), shift(part[1], z=1)
    own[1], own[3], met0, _ = lax.optimization_barrier((own[1], own[3], met0, part[0]))
    own[0] = add(both[3][0], met0[0])
    for d in (1, 3, 0):
        other[d] = shift(own[d][:ROWS], c=1)
    part1, part3 = project([(own[1], other[1]), (own[3], other[3])], tiles, [(0, carry1), (1, carry3)])
    (part0,) = project([(own[0], other[0])], tiles)
    swap = (blk & 1) == 1
    lam = jnp.where(swap, eigen[::-1], eigen)[:, :, None]
    heard = [(shift(part1[h], z=-1), shift(part3[h], z=1)) for h in range(2)]
    sums, scaled = zip(*[scale(lam, [part0[h], *heard[h]]) for h in range(2)])

    coupled = [item for d in range(4) for item in (own[d], other[d])]
    columns = []
    for h in range(2):
        piece = scaled[h]
        if h == 0:
            pieces = [piece] + [shift(piece, z=d) for d in (1, 2, 3)]
            mine = jnp.concatenate(sums, axis=2)
            mine = jnp.where(swap, mine[::-1], mine)
            projection = jnp.pad(mine, ((0, 0), (0, 512 - ROWS), (0, 0)))
            pieces[2], projection = lax.optimization_barrier((pieces[2], projection))
            arrived = pieces[1], pieces[3]
        else:
            piece, *_ = lax.optimization_barrier((piece, *arrived))
            up, down = shift(piece, z=1), shift(piece, z=-1)
            pieces = [piece, up, shift(up[:1], z=1), shift(down[1:], z=-1), down]
            pieces[0], ahead, behind = lax.optimization_barrier((pieces[0], ahead, behind))
        terms = correct(coupled, pieces)
        if h == 1:
            *terms, total = lax.optimization_barrier((*terms, total))
            columns.append(total)
        ahead, behind = shift(terms[2][:1], y=1), shift(terms[2][1:], y=-1)
        ahead = jnp.concatenate([add(terms[1][:1], ahead), terms[1][1:]])
        behind = jnp.concatenate([terms[3][:1], add(terms[3][1:], behind)])
        total = terms[0].astype(F32) + shift(ahead, y=1).astype(F32) + shift(behind, y=-1).astype(F32)
    columns.append(total)
    columns = [total[0] + shift(total[1].astype(BF), xl=1).astype(F32) for total in columns]
    return projection, jnp.concatenate(columns, axis=1)


def solution(mesh):
    placed = (
        P("leaf", "blk", None),
        P("leaf", "blk", None),
        P("leaf", "blk"),
        P("leaf", None),
        P("leaf"),
        P("leaf"),
    )
    return jax.shard_map(
        per_device,
        mesh=mesh,
        in_specs=placed,
        out_specs=(P("leaf", None, "blk"), P("leaf", "blk")),
        check_vma=False,
    )
```

```python
import jax
import jax.numpy as jnp
import numpy as np
from jax import lax
from jax.experimental import pallas as pl
from jax.experimental.pallas import tpu as pltpu
from jax.sharding import PartitionSpec as P

AXES = ("leaf", "blk")
SHAPE = (2, 4, 4, 2, 2)
ROWS = 400
LINES = 416
SPARE = 416
TILE = 512
WIDTHS = (256, 256)
ORDER = (2, 1, 3, 0)
BF = jnp.bfloat16
F32 = jnp.float32
VMEM = pl.BlockSpec(memory_space=pltpu.VMEM)
SMEM = pl.BlockSpec(memory_space=pltpu.SMEM)
HBM = pl.BlockSpec(memory_space=pltpu.HBM)
ANY = pl.BlockSpec(memory_space=pl.ANY)


def shift(value, xl=0, y=0, z=0, xh=0, c=0):
    pairs = []
    for spot in np.ndindex(*SHAPE):
        to = tuple((a + b) % n for a, b, n in zip(spot, (xl, y, z, xh, c), SHAPE))
        pairs.append((int(np.ravel_multi_index(spot, SHAPE)), int(np.ravel_multi_index(to, SHAPE))))
    return lax.ppermute(value, AXES, pairs)


def tdot(a, b):
    return lax.dot_general(a, b, (((0,), (0,)), ((), ())), preferred_element_type=F32)


def couple(which, spot, modes, stiffness):
    def kernel(spot, modes, stiffness, *outs):
        sub = spot[3] ^ which
        tag = jnp.zeros((LINES - ROWS, TILE), F32)
        if which == 0:
            places = [relative(spot[6 + (spot[3] ^ j)], spot) for j in range(2)]
            tag = tag + (places[0] + 8 * places[1]).astype(F32)
        live = lax.broadcasted_iota(jnp.int32, (ROWS, TILE), 0) < spot[4 + sub]
        turned = modes[sub].astype(F32).T[:ROWS].astype(BF)
        for k, d in enumerate(ORDER):
            first = pl.multiple_of(((spot[2] + d) & 3) * TILE, TILE)
            value = jnp.dot(turned, stiffness[sub, :, pl.ds(first, TILE)], preferred_element_type=F32)
            outs[k][0, pl.ds(0, ROWS)] = jnp.where(live, value, 0.0).astype(BF)
            outs[k][0, pl.ds(ROWS, LINES - ROWS)] = tag.astype(BF)

    return pl.pallas_call(
        kernel,
        out_shape=[jax.ShapeDtypeStruct((1, LINES, TILE), BF)] * 4,
        in_specs=[SMEM] + [VMEM] * 2,
        out_specs=[VMEM] * 4,
        compiler_params=pltpu.CompilerParams(vmem_limit_bytes=20 << 20),
        cost_estimate=pl.CostEstimate(flops=1 << 10, bytes_accessed=1 << 10, transcendentals=0),
        name="couple",
    )(spot, modes, stiffness)


def relative(separator, spot):
    return ((separator >> 2) ^ spot[0]) * 4 + ((separator - spot[1]) & 3)


def tag_of(own):
    return own[pl.ds(ROWS, 8), pl.ds(0, 128)].astype(F32)


def places_of(own):
    both = (jnp.max(tag_of(own)) * 0.5).astype(jnp.int32)
    return both & 7, both >> 3


def halves(value):
    first, out = 0, []
    for width in WIDTHS:
        out.append(value[..., first : first + width])
        first += width
    return out


def project(sides, tiles, carry=(), whole=False):
    count = len(sides)
    slots = [slot for slot, _ in carry]

    def kernel(*refs):
        sides, tiles = refs[: 2 * count], refs[2 * count : 2 * count + 8]
        carried = refs[2 * count + 8 : 2 * count + 8 + len(slots)]
        outs, (held, sems) = refs[2 * count + 8 + len(slots) : -2], refs[-2:]
        for n in range(count):
            for j, place in enumerate(places_of(sides[2 * n])):
                for k in range(8):

                    @pl.when(place == k)
                    def _():
                        pltpu.make_async_copy(tiles[k], held.at[2 * n + j], sems.at[2 * n + j]).start()

        for n in range(2 * count):
            pltpu.make_async_copy(tiles[0], held.at[n], sems.at[n]).wait()
            value = jnp.dot(sides[n][pl.ds(0, ROWS)], held[n], preferred_element_type=F32)
            if slots and slots[n // 2] == n % 2:
                value = value + carried[n // 2][0, pl.ds(0, ROWS)].astype(F32)
            if whole:
                outs[n][0, pl.ds(0, ROWS)] = value.astype(BF)
                outs[n][0, pl.ds(ROWS, SPARE - ROWS)] = jnp.zeros((SPARE - ROWS, TILE), BF)
                continue
            for h, half in enumerate(halves(value)):
                outs[n // 2 * len(WIDTHS) + h][n % 2] = half.astype(BF)

    shapes = [(1, SPARE, TILE)] * 2 if whole else [(2, ROWS, width) for width in WIDTHS] * count
    flat = pl.pallas_call(
        kernel,
        out_shape=[jax.ShapeDtypeStruct(shape, BF) for shape in shapes],
        in_specs=[VMEM] * (2 * count) + [ANY] * 8 + [VMEM] * len(slots),
        out_specs=[VMEM] * len(shapes),
        scratch_shapes=[pltpu.VMEM((2 * count, TILE, TILE), BF), pltpu.SemaphoreType.DMA((2 * count,))],
        compiler_params=pltpu.CompilerParams(vmem_limit_bytes=12 << 20),
        cost_estimate=pl.CostEstimate(flops=1 << 10, bytes_accessed=1 << 10, transcendentals=0),
        name="project",
    )(*[item for pair in sides for item in pair], *tiles, *[item for _, item in carry])
    if whole:
        return flat
    return [list(flat[n * len(WIDTHS) : (n + 1) * len(WIDTHS)]) for n in range(count)]


def scale(eigen, parts):
    def kernel(eigen, first, second, third, total, scaled):
        for j in range(2):
            value = first[j].astype(F32) + second[j].astype(F32) + third[j].astype(F32)
            total[j] = value.astype(BF)
            scaled[j] = (value * (1.0 / eigen[j, pl.ds(0, ROWS)])).astype(BF)

    return pl.pallas_call(
        kernel,
        out_shape=[jax.ShapeDtypeStruct(parts[0].shape, BF)] * 2,
        in_specs=[VMEM] * 4,
        out_specs=[VMEM] * 2,
        compiler_params=pltpu.CompilerParams(vmem_limit_bytes=10 << 20),
        cost_estimate=pl.CostEstimate(flops=1 << 10, bytes_accessed=1 << 10, transcendentals=0),
        name="scale",
    )(eigen, *parts)


def places_in(coupled):
    tags = sum(tag_of(own) * (0.5 * 64**d) for d, own in enumerate(coupled[::2]))
    places = jnp.max(tags).astype(jnp.int32)
    return [(places >> (3 * n)) & 7 for n in range(len(coupled))]


def collect(coupled, scaled):
    width, count = scaled[0].shape[2], len(coupled)

    def kernel(*refs):
        coupled, scaled, total = refs[:count], refs[count:-1], refs[-1]
        total[...] = jnp.zeros_like(total)
        for n, place in enumerate(places_in(coupled)):
            total[place] += tdot(coupled[n][pl.ds(0, ROWS)], scaled[n // 2][n % 2])

    return pl.pallas_call(
        kernel,
        out_shape=jax.ShapeDtypeStruct((8, TILE, width), F32),
        in_specs=[VMEM] * (count + len(scaled)),
        out_specs=VMEM,
        compiler_params=pltpu.CompilerParams(vmem_limit_bytes=20 << 20),
        cost_estimate=pl.CostEstimate(flops=1 << 10, bytes_accessed=1 << 10, transcendentals=0),
        name="collect",
    )(*coupled, *scaled)


def correct(total, coupled, scaled):
    width = total.shape[2]

    def kernel(total, *refs):
        coupled, scaled, outs = refs[:2], refs[2:-4], refs[-4:]
        scaled = [ref.at[j] for ref in scaled for j in range(ref.shape[0])]
        places = places_in(coupled)
        terms = [tdot(coupled[j][pl.ds(0, ROWS)], scaled[j][...]) for j in range(2)]
        for k in range(8):
            value = total[k]
            for place, term in zip(places, terms):
                value = value + jnp.where(place == k, term, 0.0)
            outs[k % 4][k // 4] = value.astype(BF)

    return pl.pallas_call(
        kernel,
        out_shape=[jax.ShapeDtypeStruct((2, TILE, width), BF)] * 4,
        in_specs=[VMEM] * (3 + len(scaled)),
        out_specs=[VMEM] * 4,
        compiler_params=pltpu.CompilerParams(vmem_limit_bytes=20 << 20),
        cost_estimate=pl.CostEstimate(flops=1 << 10, bytes_accessed=1 << 10, transcendentals=0),
        name="correct",
    )(total, *coupled, *scaled)


def add(a, b):
    return (a.astype(F32) + b.astype(F32)).astype(BF)


def per_device(stiffness, modes, basis, eigen, counts, ancestry):
    leaf, blk = lax.axis_index("leaf"), lax.axis_index("blk")
    spot = jnp.stack([leaf >> 4, (leaf >> 2) & 3, leaf & 3, blk & 1, counts[0], counts[1], ancestry[0], ancestry[1]])

    crossed = shift(basis, xl=1)
    above, below = shift(basis, y=-1), shift(basis, y=1)
    away = couple(1, spot, modes, stiffness)
    came = [shift(piece, c=1) for piece in away]
    late, crossed = lax.optimization_barrier((spot, crossed))
    kept = couple(0, late, modes, stiffness)
    both = [add(*pair) for pair in zip(kept, came)]
    crossed, _ = lax.optimization_barrier((crossed, both[0]))
    cabove, cbelow = shift(crossed, y=-1), shift(crossed, y=1)
    met2, met13, met0 = (shift(item, xh=1) for item in (both[0], jnp.concatenate(both[1:3]), both[3]))
    met2, above, below = lax.optimization_barrier((met2, above, below))
    own, other = {}, {}
    own[2] = shift(add(both[0][0], met2[0]), z=2)
    mid = TILE // 2
    far1 = shift(jnp.stack([above[:mid], cabove[:mid]]), y=-1)
    far2 = shift(jnp.stack([below[mid:], cbelow[mid:]]), y=1)
    other[2] = shift(own[2][:ROWS], c=1)
    met13, other[2], far1, far2 = lax.optimization_barrier((met13, other[2], far1, far2))
    own[1] = shift(add(both[1][0], met13[0]), z=1)
    own[3] = shift(add(both[2][0], met13[1]), z=3)
    far = jnp.concatenate([far1, far2], axis=1)
    tiles = [basis, above, far[0], below, crossed, cabove, far[1], cbelow]
    part = project([(own[2], other[2])], tiles, whole=True)
    carry1, carry3 = shift(part[0], z=-1), shift(part[1], z=1)
    own[1], own[3], met0, _ = lax.optimization_barrier((own[1], own[3], met0, part[0]))
    own[0] = add(both[3][0], met0[0])
    for d in (1, 3, 0):
        other[d] = shift(own[d][:ROWS], c=1)
    part1, part3 = project([(own[1], other[1]), (own[3], other[3])], tiles, [(0, carry1), (1, carry3)])
    (part0,) = project([(own[0], other[0])], tiles)
    swap = (blk & 1) == 1
    lam = jnp.where(swap, eigen[::-1], eigen)[:, :, None]
    coupled = [item for d in (0, 1, 3) for item in (own[d], other[d])]
    columns = []
    sums = []
    heard = shift(part1[0], z=-1), shift(part3[0], z=1)
    for h in range(2):
        mine, piece = scale(lam, [part0[h], *heard])
        sums.append(mine)
        up, down = shift(piece, z=1), shift(piece, z=-1)
        far = [shift(up[:1], z=1), shift(down[1:], z=-1)]
        if h == 0:
            part1[1], part3[1], _ = lax.optimization_barrier((part1[1], part3[1], up))
            heard = shift(part1[1], z=-1), shift(part3[1], z=1)
        else:
            mine = jnp.concatenate(sums, axis=2)
            mine = jnp.where(swap, mine[::-1], mine)
            projection = jnp.pad(mine, ((0, 0), (0, 512 - ROWS), (0, 0)))
            far[0], projection = lax.optimization_barrier((far[0], projection))
            piece, ahead, behind = lax.optimization_barrier((piece, ahead, behind))
        terms = correct(collect(coupled, [piece, up, down]), [own[2], other[2]], far)
        if h == 1:
            *terms, total = lax.optimization_barrier((*terms, total))
            columns.append(total)
        ahead, behind = shift(terms[2][:1], y=1), shift(terms[2][1:], y=-1)
        ahead, behind, *_ = lax.optimization_barrier((ahead, behind, *heard))
        ahead = jnp.concatenate([add(terms[1][:1], ahead), terms[1][1:]])
        behind = jnp.concatenate([terms[3][:1], add(terms[3][1:], behind)])
        total = terms[0].astype(F32) + shift(ahead, y=1).astype(F32) + shift(behind, y=-1).astype(F32)
    columns.append(total)
    columns = [total[0] + shift(total[1].astype(BF), xl=1).astype(F32) for total in columns]
    return projection, jnp.concatenate(columns, axis=1)


def solution(mesh):
    placed = (
        P("leaf", "blk", None),
        P("leaf", "blk", None),
        P("leaf", "blk"),
        P("leaf", None),
        P("leaf"),
        P("leaf"),
    )
    return jax.shard_map(
        per_device,
        mesh=mesh,
        in_specs=placed,
        out_specs=(P("leaf", None, "blk"), P("leaf", "blk")),
        check_vma=False,
    )
```

```python
import jax
import jax.numpy as jnp
import numpy as np
from jax import lax
from jax.experimental import pallas as pl
from jax.experimental.pallas import tpu as pltpu
from jax.sharding import PartitionSpec as P

AXES = ("leaf", "blk")
SHAPE = (2, 4, 4, 2, 2)
ROWS = 400
LINES = 416
SPARE = 416
TILE = 512
WIDTHS = (256, 256)
ORDER = (2, 1, 3, 0)
BF = jnp.bfloat16
F32 = jnp.float32
VMEM = pl.BlockSpec(memory_space=pltpu.VMEM)
SMEM = pl.BlockSpec(memory_space=pltpu.SMEM)
HBM = pl.BlockSpec(memory_space=pltpu.HBM)
ANY = pl.BlockSpec(memory_space=pl.ANY)


def shift(value, xl=0, y=0, z=0, xh=0, c=0):
    pairs = []
    for spot in np.ndindex(*SHAPE):
        to = tuple((a + b) % n for a, b, n in zip(spot, (xl, y, z, xh, c), SHAPE))
        pairs.append((int(np.ravel_multi_index(spot, SHAPE)), int(np.ravel_multi_index(to, SHAPE))))
    return lax.ppermute(value, AXES, pairs)


def tdot(a, b):
    return lax.dot_general(a, b, (((0,), (0,)), ((), ())), preferred_element_type=F32)


def couple(which, spot, modes, stiffness):
    def kernel(spot, modes, stiffness, *outs):
        sub = spot[3] ^ which
        tag = jnp.zeros((LINES - ROWS, TILE), F32)
        if which == 0:
            places = [relative(spot[6 + (spot[3] ^ j)], spot) for j in range(2)]
            tag = tag + (places[0] + 8 * places[1]).astype(F32)
        live = lax.broadcasted_iota(jnp.int32, (ROWS, TILE), 0) < spot[4 + sub]
        turned = modes[sub].astype(F32).T[:ROWS].astype(BF)
        for k, d in enumerate(ORDER):
            first = pl.multiple_of(((spot[2] + d) & 3) * TILE, TILE)
            value = jnp.dot(turned, stiffness[sub, :, pl.ds(first, TILE)], preferred_element_type=F32)
            outs[k][0, pl.ds(0, ROWS)] = jnp.where(live, value, 0.0).astype(BF)
            outs[k][0, pl.ds(ROWS, LINES - ROWS)] = tag.astype(BF)

    return pl.pallas_call(
        kernel,
        out_shape=[jax.ShapeDtypeStruct((1, LINES, TILE), BF)] * 4,
        in_specs=[SMEM] + [VMEM] * 2,
        out_specs=[VMEM] * 4,
        compiler_params=pltpu.CompilerParams(vmem_limit_bytes=20 << 20),
        cost_estimate=pl.CostEstimate(flops=1 << 10, bytes_accessed=1 << 10, transcendentals=0),
        name="couple",
    )(spot, modes, stiffness)


def relative(separator, spot):
    return ((separator >> 2) ^ spot[0]) * 4 + ((separator - spot[1]) & 3)


def tag_of(own):
    return own[pl.ds(ROWS, 8), pl.ds(0, 128)].astype(F32)


def places_of(own):
    both = (jnp.max(tag_of(own)) * 0.5).astype(jnp.int32)
    return both & 7, both >> 3


def halves(value):
    first, out = 0, []
    for width in WIDTHS:
        out.append(value[..., first : first + width])
        first += width
    return out


def pick(owns, tiles):
    count = len(owns)

    def kernel(*refs):
        owns, tiles, held, sems = refs[:count], refs[count : count + 8], refs[-2], refs[-1]
        for n, own in enumerate(owns):
            for j, place in enumerate(places_of(own)):
                for k in range(8):

                    @pl.when(place == k)
                    def _():
                        pltpu.make_async_copy(tiles[k], held.at[2 * n + j], sems.at[2 * n + j]).start()

        for n in range(2 * count):
            pltpu.make_async_copy(tiles[0], held.at[n], sems.at[n]).wait()

    return pl.pallas_call(
        kernel,
        out_shape=jax.ShapeDtypeStruct((2 * count, TILE, TILE), BF),
        in_specs=[VMEM] * count + [ANY] * 8,
        out_specs=VMEM,
        scratch_shapes=[pltpu.SemaphoreType.DMA((2 * count,))],
        compiler_params=pltpu.CompilerParams(vmem_limit_bytes=12 << 20),
        cost_estimate=pl.CostEstimate(flops=1 << 10, bytes_accessed=1 << 10, transcendentals=0),
        name="pick",
    )(*owns, *tiles)


def project(sides, held, carry=(), whole=False):
    count = len(sides)
    slots = [slot for slot, _ in carry]

    def kernel(held, *refs):
        sides, carried, outs = refs[: 2 * count], refs[2 * count : 2 * count + len(slots)], refs[2 * count + len(slots) :]
        for n in range(2 * count):
            value = jnp.dot(sides[n][pl.ds(0, ROWS)], held[n], preferred_element_type=F32)
            if slots and slots[n // 2] == n % 2:
                value = value + carried[n // 2][0, pl.ds(0, ROWS)].astype(F32)
            if whole:
                outs[n][0, pl.ds(0, ROWS)] = value.astype(BF)
                outs[n][0, pl.ds(ROWS, SPARE - ROWS)] = jnp.zeros((SPARE - ROWS, TILE), BF)
                continue
            for h, half in enumerate(halves(value)):
                outs[n // 2 * len(WIDTHS) + h][n % 2] = half.astype(BF)

    shapes = [(1, SPARE, TILE)] * 2 if whole else [(2, ROWS, width) for width in WIDTHS] * count
    flat = pl.pallas_call(
        kernel,
        out_shape=[jax.ShapeDtypeStruct(shape, BF) for shape in shapes],
        in_specs=[VMEM] * (1 + 2 * count + len(slots)),
        out_specs=[VMEM] * len(shapes),
        compiler_params=pltpu.CompilerParams(vmem_limit_bytes=12 << 20),
        cost_estimate=pl.CostEstimate(flops=1 << 10, bytes_accessed=1 << 10, transcendentals=0),
        name="project",
    )(held, *[item for pair in sides for item in pair], *[item for _, item in carry])
    if whole:
        return flat
    return [list(flat[n * len(WIDTHS) : (n + 1) * len(WIDTHS)]) for n in range(count)]


def scale(eigen, parts):
    def kernel(eigen, first, second, third, total, scaled):
        for j in range(2):
            value = first[j].astype(F32) + second[j].astype(F32) + third[j].astype(F32)
            total[j] = value.astype(BF)
            scaled[j] = (value * (1.0 / eigen[j, pl.ds(0, ROWS)])).astype(BF)

    return pl.pallas_call(
        kernel,
        out_shape=[jax.ShapeDtypeStruct(parts[0].shape, BF)] * 2,
        in_specs=[VMEM] * 4,
        out_specs=[VMEM] * 2,
        compiler_params=pltpu.CompilerParams(vmem_limit_bytes=10 << 20),
        cost_estimate=pl.CostEstimate(flops=1 << 10, bytes_accessed=1 << 10, transcendentals=0),
        name="scale",
    )(eigen, *parts)


def places_in(coupled):
    tags = sum(tag_of(own) * (0.5 * 64**d) for d, own in enumerate(coupled[::2]))
    places = jnp.max(tags).astype(jnp.int32)
    return [(places >> (3 * n)) & 7 for n in range(len(coupled))]


def collect(coupled, scaled):
    width, count = scaled[0].shape[2], len(coupled)

    def kernel(*refs):
        coupled, scaled, total = refs[:count], refs[count:-1], refs[-1]
        total[...] = jnp.zeros_like(total)
        for n, place in enumerate(places_in(coupled)):
            total[place] += tdot(coupled[n][pl.ds(0, ROWS)], scaled[n // 2][n % 2])

    return pl.pallas_call(
        kernel,
        out_shape=jax.ShapeDtypeStruct((8, TILE, width), F32),
        in_specs=[VMEM] * (count + len(scaled)),
        out_specs=VMEM,
        compiler_params=pltpu.CompilerParams(vmem_limit_bytes=20 << 20),
        cost_estimate=pl.CostEstimate(flops=1 << 10, bytes_accessed=1 << 10, transcendentals=0),
        name="collect",
    )(*coupled, *scaled)


def correct(total, coupled, scaled):
    width = total.shape[2]

    def kernel(total, *refs):
        coupled, scaled, outs = refs[:2], refs[2:-4], refs[-4:]
        scaled = [ref.at[j] for ref in scaled for j in range(ref.shape[0])]
        places = places_in(coupled)
        terms = [tdot(coupled[j][pl.ds(0, ROWS)], scaled[j][...]) for j in range(2)]
        for k in range(8):
            value = total[k]
            for place, term in zip(places, terms):
                value = value + jnp.where(place == k, term, 0.0)
            outs[k % 4][k // 4] = value.astype(BF)

    return pl.pallas_call(
        kernel,
        out_shape=[jax.ShapeDtypeStruct((2, TILE, width), BF)] * 4,
        in_specs=[VMEM] * (3 + len(scaled)),
        out_specs=[VMEM] * 4,
        compiler_params=pltpu.CompilerParams(vmem_limit_bytes=20 << 20),
        cost_estimate=pl.CostEstimate(flops=1 << 10, bytes_accessed=1 << 10, transcendentals=0),
        name="correct",
    )(total, *coupled, *scaled)


def add(a, b):
    return (a.astype(F32) + b.astype(F32)).astype(BF)


def per_device(stiffness, modes, basis, eigen, counts, ancestry):
    leaf, blk = lax.axis_index("leaf"), lax.axis_index("blk")
    spot = jnp.stack([leaf >> 4, (leaf >> 2) & 3, leaf & 3, blk & 1, counts[0], counts[1], ancestry[0], ancestry[1]])

    crossed = shift(basis, xl=1)
    above, below = shift(basis, y=-1), shift(basis, y=1)
    away = couple(1, spot, modes, stiffness)
    came = [shift(piece, c=1) for piece in away]
    late, crossed = lax.optimization_barrier((spot, crossed))
    kept = couple(0, late, modes, stiffness)
    both = [add(*pair) for pair in zip(kept, came)]
    crossed, _ = lax.optimization_barrier((crossed, both[0]))
    cabove, cbelow = shift(crossed, y=-1), shift(crossed, y=1)
    met2, met13, met0 = (shift(item, xh=1) for item in (both[0], jnp.concatenate(both[1:3]), both[3]))
    met2, above, below = lax.optimization_barrier((met2, above, below))
    own, other = {}, {}
    own[2] = shift(add(both[0][0], met2[0]), z=2)
    mid = TILE // 2
    far1 = shift(jnp.stack([above[:mid], cabove[:mid]]), y=-1)
    far2 = shift(jnp.stack([below[mid:], cbelow[mid:]]), y=1)
    other[2] = shift(own[2][:ROWS], c=1)
    met13, other[2], far1, far2 = lax.optimization_barrier((met13, other[2], far1, far2))
    own[1] = shift(add(both[1][0], met13[0]), z=1)
    own[3] = shift(add(both[2][0], met13[1]), z=3)
    far = jnp.concatenate([far1, far2], axis=1)
    tiles = [basis, above, far[0], below, crossed, cabove, far[1], cbelow]
    part = project([(own[2], other[2])], pick([own[2]], tiles), whole=True)
    carry1, carry3 = shift(part[0], z=-1), shift(part[1], z=1)
    own[1], own[3], met0, _ = lax.optimization_barrier((own[1], own[3], met0, part[0]))
    own[0] = add(both[3][0], met0[0])
    for d in (1, 3, 0):
        other[d] = shift(own[d][:ROWS], c=1)
    held = pick([own[1], own[3]], tiles)
    part1, part3 = project([(own[1], other[1]), (own[3], other[3])], held, [(0, carry1), (1, carry3)])
    (part0,) = project([(own[0], other[0])], pick([own[0]], tiles))
    swap = (blk & 1) == 1
    lam = jnp.where(swap, eigen[::-1], eigen)[:, :, None]
    coupled = [item for d in (0, 1, 3) for item in (own[d], other[d])]
    columns = []
    sums = []
    heard = shift(part1[0], z=-1), shift(part3[0], z=1)
    for h in range(2):
        mine, piece = scale(lam, [part0[h], *heard])
        sums.append(mine)
        up, down = shift(piece, z=1), shift(piece, z=-1)
        far = [shift(up[:1], z=1), shift(down[1:], z=-1)]
        if h == 0:
            part1[1], part3[1], _ = lax.optimization_barrier((part1[1], part3[1], up))
            heard = shift(part1[1], z=-1), shift(part3[1], z=1)
        else:
            mine = jnp.concatenate(sums, axis=2)
            mine = jnp.where(swap, mine[::-1], mine)
            projection = jnp.pad(mine, ((0, 0), (0, 512 - ROWS), (0, 0)))
            far[0], projection = lax.optimization_barrier((far[0], projection))
            piece, ahead, behind = lax.optimization_barrier((piece, ahead, behind))
        terms = correct(collect(coupled, [piece, up, down]), [own[2], other[2]], far)
        if h == 1:
            *terms, total = lax.optimization_barrier((*terms, total))
            columns.append(total)
        ahead, behind = shift(terms[2][:1], y=1), shift(terms[2][1:], y=-1)
        ahead, behind, *_ = lax.optimization_barrier((ahead, behind, *heard))
        ahead = jnp.concatenate([add(terms[1][:1], ahead), terms[1][1:]])
        behind = jnp.concatenate([terms[3][:1], add(terms[3][1:], behind)])
        total = terms[0].astype(F32) + shift(ahead, y=1).astype(F32) + shift(behind, y=-1).astype(F32)
    columns.append(total)
    columns = [total[0] + shift(total[1].astype(BF), xl=1).astype(F32) for total in columns]
    return projection, jnp.concatenate(columns, axis=1)


def solution(mesh):
    placed = (
        P("leaf", "blk", None),
        P("leaf", "blk", None),
        P("leaf", "blk"),
        P("leaf", None),
        P("leaf"),
        P("leaf"),
    )
    return jax.shard_map(
        per_device,
        mesh=mesh,
        in_specs=placed,
        out_specs=(P("leaf", None, "blk"), P("leaf", "blk")),
        check_vma=False,
    )
```

```python
import jax
import jax.numpy as jnp
import numpy as np
from jax import lax
from jax.experimental import pallas as pl
from jax.experimental.pallas import tpu as pltpu
from jax.sharding import PartitionSpec as P

AXES = ("leaf", "blk")
SHAPE = (2, 4, 4, 2, 2)
ROWS = 400
LINES = 416
SPARE = 416
TILE = 512
HALVES = ((0, 256), (256, 256))
ORDER = (2, 1, 3, 0)
BF = jnp.bfloat16
F32 = jnp.float32
VMEM = pl.BlockSpec(memory_space=pltpu.VMEM)
SMEM = pl.BlockSpec(memory_space=pltpu.SMEM)
HBM = pl.BlockSpec(memory_space=pltpu.HBM)
ANY = pl.BlockSpec(memory_space=pl.ANY)


def shift(value, xl=0, y=0, z=0, xh=0, c=0):
    pairs = []
    for spot in np.ndindex(*SHAPE):
        to = tuple((a + b) % n for a, b, n in zip(spot, (xl, y, z, xh, c), SHAPE))
        pairs.append((int(np.ravel_multi_index(spot, SHAPE)), int(np.ravel_multi_index(to, SHAPE))))
    return lax.ppermute(value, AXES, pairs)


def tdot(a, b):
    return lax.dot_general(a, b, (((0,), (0,)), ((), ())), preferred_element_type=F32)


def couple(which, spot, modes, stiffness):
    def kernel(spot, modes, stiffness, *outs):
        sub = spot[3] ^ which
        tag = jnp.zeros((LINES - ROWS, TILE), F32)
        if which == 0:
            places = [relative(spot[6 + (spot[3] ^ j)], spot) for j in range(2)]
            tag = tag + (places[0] + 8 * places[1]).astype(F32)
        live = lax.broadcasted_iota(jnp.int32, (ROWS, TILE), 0) < spot[4 + sub]
        turned = modes[sub].astype(F32).T[:ROWS].astype(BF)
        for k, d in enumerate(ORDER):
            first = pl.multiple_of(((spot[2] + d) & 3) * TILE, TILE)
            value = jnp.dot(turned, stiffness[sub, :, pl.ds(first, TILE)], preferred_element_type=F32)
            outs[k][0, pl.ds(0, ROWS)] = jnp.where(live, value, 0.0).astype(BF)
            outs[k][0, pl.ds(ROWS, LINES - ROWS)] = tag.astype(BF)

    return pl.pallas_call(
        kernel,
        out_shape=[jax.ShapeDtypeStruct((1, LINES, TILE), BF)] * 4,
        in_specs=[SMEM] + [VMEM] * 2,
        out_specs=[VMEM] * 4,
        compiler_params=pltpu.CompilerParams(vmem_limit_bytes=20 << 20),
        cost_estimate=pl.CostEstimate(flops=1 << 10, bytes_accessed=1 << 10, transcendentals=0),
        name="couple",
    )(spot, modes, stiffness)


def relative(separator, spot):
    return ((separator >> 2) ^ spot[0]) * 4 + ((separator - spot[1]) & 3)


def tag_of(own):
    return own[pl.ds(ROWS, LINES - ROWS), pl.ds(0, 128)].astype(F32)


def places_of(own):
    both = (jnp.max(tag_of(own)) * 0.5).astype(jnp.int32)
    return both & 7, both >> 3


def pick(owns, tiles):
    count = len(owns)

    def kernel(*refs):
        owns, tiles, held, sems = refs[:count], refs[count : count + 8], refs[-2], refs[-1]
        for n, own in enumerate(owns):
            for j, place in enumerate(places_of(own)):
                for k in range(8):

                    @pl.when(place == k)
                    def _():
                        pltpu.make_async_copy(tiles[k], held.at[2 * n + j], sems.at[2 * n + j]).start()

        for n in range(2 * count):
            pltpu.make_async_copy(tiles[0], held.at[n], sems.at[n]).wait()

    return pl.pallas_call(
        kernel,
        out_shape=jax.ShapeDtypeStruct((2 * count, TILE, TILE), BF),
        in_specs=[VMEM] * count + [ANY] * 8,
        out_specs=VMEM,
        scratch_shapes=[pltpu.SemaphoreType.DMA((2 * count,))],
        compiler_params=pltpu.CompilerParams(vmem_limit_bytes=12 << 20),
        cost_estimate=pl.CostEstimate(flops=1 << 10, bytes_accessed=1 << 10, transcendentals=0),
        name="pick",
    )(*owns, *tiles)


def project(sides, held, carry=(), columns=(0, TILE)):
    count = len(sides)
    slots = [slot for slot, _ in carry]
    first, width = columns
    whole = width == TILE

    def kernel(held, *refs):
        sides, carried, outs = refs[: 2 * count], refs[2 * count : 2 * count + len(slots)], refs[2 * count + len(slots) :]
        for n in range(2 * count):
            tile = held[n, :, pl.ds(first, width)]
            value = jnp.dot(sides[n][pl.ds(0, ROWS)], tile, preferred_element_type=F32)
            if slots and slots[n // 2] == n % 2:
                value = value + carried[n // 2][0, pl.ds(0, ROWS), pl.ds(first, width)].astype(F32)
            if whole:
                outs[n][0, pl.ds(0, ROWS)] = value.astype(BF)
                outs[n][0, pl.ds(ROWS, SPARE - ROWS)] = jnp.zeros((SPARE - ROWS, TILE), BF)
            else:
                outs[n // 2][n % 2] = value.astype(BF)

    shapes = [(1, SPARE, TILE)] * 2 if whole else [(2, ROWS, width)] * count
    return pl.pallas_call(
        kernel,
        out_shape=[jax.ShapeDtypeStruct(shape, BF) for shape in shapes],
        in_specs=[VMEM] * (1 + 2 * count + len(slots)),
        out_specs=[VMEM] * len(shapes),
        compiler_params=pltpu.CompilerParams(vmem_limit_bytes=12 << 20),
        cost_estimate=pl.CostEstimate(flops=1 << 10, bytes_accessed=1 << 10, transcendentals=0),
        name="project",
    )(held, *[item for pair in sides for item in pair], *[item for _, item in carry])


def scale(eigen, parts):
    def kernel(eigen, first, second, third, total, scaled):
        for j in range(2):
            value = first[j].astype(F32) + second[j].astype(F32) + third[j].astype(F32)
            total[j] = value.astype(BF)
            scaled[j] = (value * (1.0 / eigen[j, pl.ds(0, ROWS)])).astype(BF)

    return pl.pallas_call(
        kernel,
        out_shape=[jax.ShapeDtypeStruct(parts[0].shape, BF)] * 2,
        in_specs=[VMEM] * 4,
        out_specs=[VMEM] * 2,
        compiler_params=pltpu.CompilerParams(vmem_limit_bytes=10 << 20),
        cost_estimate=pl.CostEstimate(flops=1 << 10, bytes_accessed=1 << 10, transcendentals=0),
        name="scale",
    )(eigen, *parts)


def places_in(coupled):
    tags = sum(tag_of(own) * (0.5 * 64**d) for d, own in enumerate(coupled[::2]))
    places = jnp.max(tags).astype(jnp.int32)
    return [(places >> (3 * n)) & 7 for n in range(len(coupled))]


def collect(coupled, scaled):
    width, count = scaled[0].shape[2], len(coupled)

    def kernel(*refs):
        coupled, scaled, total = refs[:count], refs[count:-1], refs[-1]
        total[...] = jnp.zeros_like(total)
        for n, place in enumerate(places_in(coupled)):
            total[place] += tdot(coupled[n][pl.ds(0, ROWS)], scaled[n // 2][n % 2])

    return pl.pallas_call(
        kernel,
        out_shape=jax.ShapeDtypeStruct((8, TILE, width), F32),
        in_specs=[VMEM] * (count + len(scaled)),
        out_specs=VMEM,
        compiler_params=pltpu.CompilerParams(vmem_limit_bytes=20 << 20),
        cost_estimate=pl.CostEstimate(flops=1 << 10, bytes_accessed=1 << 10, transcendentals=0),
        name="collect",
    )(*coupled, *scaled)


def correct(total, coupled, scaled):
    width = total.shape[2]

    def kernel(total, *refs):
        coupled, scaled, outs = refs[:2], refs[2:-4], refs[-4:]
        scaled = [ref.at[j] for ref in scaled for j in range(ref.shape[0])]
        places = places_in(coupled)
        terms = [tdot(coupled[j][pl.ds(0, ROWS)], scaled[j][...]) for j in range(2)]
        for k in range(8):
            value = total[k]
            for place, term in zip(places, terms):
                value = value + jnp.where(place == k, term, 0.0)
            outs[k % 4][k // 4] = value.astype(BF)

    return pl.pallas_call(
        kernel,
        out_shape=[jax.ShapeDtypeStruct((2, TILE, width), BF)] * 4,
        in_specs=[VMEM] * (3 + len(scaled)),
        out_specs=[VMEM] * 4,
        compiler_params=pltpu.CompilerParams(vmem_limit_bytes=20 << 20),
        cost_estimate=pl.CostEstimate(flops=1 << 10, bytes_accessed=1 << 10, transcendentals=0),
        name="correct",
    )(total, *coupled, *scaled)


def add(a, b):
    return (a.astype(F32) + b.astype(F32)).astype(BF)


def per_device(stiffness, modes, basis, eigen, counts, ancestry):
    leaf, blk = lax.axis_index("leaf"), lax.axis_index("blk")
    spot = jnp.stack([leaf >> 4, (leaf >> 2) & 3, leaf & 3, blk & 1, counts[0], counts[1], ancestry[0], ancestry[1]])

    crossed = shift(basis, xl=1)
    above, below = shift(basis, y=-1), shift(basis, y=1)
    away = couple(1, spot, modes, stiffness)
    came = [shift(piece, c=1) for piece in away]
    late, crossed = lax.optimization_barrier((spot, crossed))
    kept = couple(0, late, modes, stiffness)
    both = [add(*pair) for pair in zip(kept, came)]
    crossed, _ = lax.optimization_barrier((crossed, both[0]))
    cabove, cbelow = shift(crossed, y=-1), shift(crossed, y=1)
    met2, met13, met0 = (shift(item, xh=1) for item in (both[0], jnp.concatenate(both[1:3]), both[3]))
    met2, above, below = lax.optimization_barrier((met2, above, below))
    own, other = {}, {}
    own[2] = shift(add(both[0][0], met2[0]), z=2)
    mid = TILE // 2
    far1 = shift(jnp.stack([above[:mid], cabove[:mid]]), y=-1)
    far2 = shift(jnp.stack([below[mid:], cbelow[mid:]]), y=1)
    other[2] = shift(own[2][:ROWS], c=1)
    met13, other[2], far1, far2 = lax.optimization_barrier((met13, other[2], far1, far2))
    own[1] = shift(add(both[1][0], met13[0]), z=1)
    own[3] = shift(add(both[2][0], met13[1]), z=3)
    far = jnp.concatenate([far1, far2], axis=1)
    tiles = [basis, above, far[0], below, crossed, cabove, far[1], cbelow]
    part = project([(own[2], other[2])], pick([own[2]], tiles))
    carry1, carry3 = shift(part[0], z=-1), shift(part[1], z=1)
    own[1], own[3], met0, _ = lax.optimization_barrier((own[1], own[3], met0, part[0]))
    own[0] = add(both[3][0], met0[0])
    for d in (1, 3, 0):
        other[d] = shift(own[d][:ROWS], c=1)
    held, held0 = pick([own[1], own[3]], tiles), pick([own[0]], tiles)
    part0, part1, part3 = {}, {}, {}
    for h, columns in enumerate(HALVES):
        pairs = [(own[1], other[1]), (own[3], other[3])]
        part1[h], part3[h] = project(pairs, held, [(0, carry1), (1, carry3)], columns)
        (part0[h],) = project([(own[0], other[0])], held0, (), columns)
    swap = (blk & 1) == 1
    lam = jnp.where(swap, eigen[::-1], eigen)[:, :, None]
    coupled = [item for d in (0, 1, 3) for item in (own[d], other[d])]
    columns = []
    sums = []
    heard = shift(part1[0], z=-1), shift(part3[0], z=1)
    for h in range(2):
        mine, piece = scale(lam, [part0[h], *heard])
        sums.append(mine)
        up, down = shift(piece, z=1), shift(piece, z=-1)
        far = [shift(up[:1], z=1), shift(down[1:], z=-1)]
        if h == 0:
            part1[1], part3[1], _ = lax.optimization_barrier((part1[1], part3[1], up))
            heard = shift(part1[1], z=-1), shift(part3[1], z=1)
        else:
            mine = jnp.concatenate(sums, axis=2)
            mine = jnp.where(swap, mine[::-1], mine)
            projection = jnp.pad(mine, ((0, 0), (0, 512 - ROWS), (0, 0)))
            far[0], projection = lax.optimization_barrier((far[0], projection))
            piece, ahead, behind = lax.optimization_barrier((piece, ahead, behind))
        terms = correct(collect(coupled, [piece, up, down]), [own[2], other[2]], far)
        if h == 1:
            *terms, total = lax.optimization_barrier((*terms, total))
            columns.append(total)
        ahead, behind = shift(terms[2][:1], y=1), shift(terms[2][1:], y=-1)
        ahead, behind, *_ = lax.optimization_barrier((ahead, behind, *heard))
        ahead = jnp.concatenate([add(terms[1][:1], ahead), terms[1][1:]])
        behind = jnp.concatenate([terms[3][:1], add(terms[3][1:], behind)])
        total = terms[0].astype(F32) + shift(ahead, y=1).astype(F32) + shift(behind, y=-1).astype(F32)
    columns.append(total)
    columns = [total[0] + shift(total[1].astype(BF), xl=1).astype(F32) for total in columns]
    return projection, jnp.concatenate(columns, axis=1)


def solution(mesh):
    placed = (
        P("leaf", "blk", None),
        P("leaf", "blk", None),
        P("leaf", "blk"),
        P("leaf", None),
        P("leaf"),
        P("leaf"),
    )
    return jax.shard_map(
        per_device,
        mesh=mesh,
        in_specs=placed,
        out_specs=(P("leaf", None, "blk"), P("leaf", "blk")),
        check_vma=False,
    )
```

```python
import jax
import jax.numpy as jnp
import numpy as np
from jax import lax
from jax.experimental import pallas as pl
from jax.experimental.pallas import tpu as pltpu
from jax.sharding import PartitionSpec as P

AXES = ("leaf", "blk")
SHAPE = (2, 4, 4, 2, 2)
ROWS = 400
LINES = 416
SPARE = 416
TILE = 512
WIDTHS = (256, 256)
ORDER = (2, 1, 3, 0)
BF = jnp.bfloat16
F32 = jnp.float32
VMEM = pl.BlockSpec(memory_space=pltpu.VMEM)
SMEM = pl.BlockSpec(memory_space=pltpu.SMEM)
HBM = pl.BlockSpec(memory_space=pltpu.HBM)
ANY = pl.BlockSpec(memory_space=pl.ANY)


def shift(value, xl=0, y=0, z=0, xh=0, c=0):
    pairs = []
    for spot in np.ndindex(*SHAPE):
        to = tuple((a + b) % n for a, b, n in zip(spot, (xl, y, z, xh, c), SHAPE))
        pairs.append((int(np.ravel_multi_index(spot, SHAPE)), int(np.ravel_multi_index(to, SHAPE))))
    return lax.ppermute(value, AXES, pairs)


def tdot(a, b):
    return lax.dot_general(a, b, (((0,), (0,)), ((), ())), preferred_element_type=F32)


def couple(which, spot, modes, stiffness):
    def kernel(spot, modes, stiffness, *outs):
        sub = spot[3] ^ which
        tag = jnp.zeros((LINES - ROWS, TILE), F32)
        if which == 0:
            places = [relative(spot[6 + (spot[3] ^ j)], spot) for j in range(2)]
            tag = tag + (places[0] + 8 * places[1]).astype(F32)
        live = lax.broadcasted_iota(jnp.int32, (ROWS, TILE), 0) < spot[4 + sub]
        turned = modes[sub].astype(F32).T[:ROWS].astype(BF)
        for k, d in enumerate(ORDER):
            first = pl.multiple_of(((spot[2] + d) & 3) * TILE, TILE)
            value = jnp.dot(turned, stiffness[sub, :, pl.ds(first, TILE)], preferred_element_type=F32)
            outs[k][0, pl.ds(0, ROWS)] = jnp.where(live, value, 0.0).astype(BF)
            outs[k][0, pl.ds(ROWS, LINES - ROWS)] = tag.astype(BF)

    return pl.pallas_call(
        kernel,
        out_shape=[jax.ShapeDtypeStruct((1, LINES, TILE), BF)] * 4,
        in_specs=[SMEM] + [VMEM] * 2,
        out_specs=[VMEM] * 4,
        compiler_params=pltpu.CompilerParams(vmem_limit_bytes=20 << 20),
        cost_estimate=pl.CostEstimate(flops=1 << 10, bytes_accessed=1 << 10, transcendentals=0),
        name="couple",
    )(spot, modes, stiffness)


def relative(separator, spot):
    return ((separator >> 2) ^ spot[0]) * 4 + ((separator - spot[1]) & 3)


def tag_of(own):
    return own[pl.ds(ROWS, LINES - ROWS), pl.ds(0, 128)].astype(F32)


def places_of(own):
    both = (jnp.max(tag_of(own)) * 0.5).astype(jnp.int32)
    return both & 7, both >> 3


def halves(value):
    first, out = 0, []
    for width in WIDTHS:
        out.append(value[..., first : first + width])
        first += width
    return out


def pick(owns, tiles):
    count = len(owns)

    def kernel(*refs):
        owns, tiles, held, sems = refs[:count], refs[count : count + 8], refs[-2], refs[-1]
        for n, own in enumerate(owns):
            for j, place in enumerate(places_of(own)):
                for k in range(8):

                    @pl.when(place == k)
                    def _():
                        pltpu.make_async_copy(tiles[k], held.at[2 * n + j], sems.at[2 * n + j]).start()

        for n in range(2 * count):
            pltpu.make_async_copy(tiles[0], held.at[n], sems.at[n]).wait()

    return pl.pallas_call(
        kernel,
        out_shape=jax.ShapeDtypeStruct((2 * count, TILE, TILE), BF),
        in_specs=[VMEM] * count + [ANY] * 8,
        out_specs=VMEM,
        scratch_shapes=[pltpu.SemaphoreType.DMA((2 * count,))],
        compiler_params=pltpu.CompilerParams(vmem_limit_bytes=12 << 20),
        cost_estimate=pl.CostEstimate(flops=1 << 10, bytes_accessed=1 << 10, transcendentals=0),
        name="pick",
    )(*owns, *tiles)


def project(sides, held, carry=(), whole=False):
    count = len(sides)
    slots = [slot for slot, _ in carry]

    def kernel(held, *refs):
        sides, carried, outs = refs[: 2 * count], refs[2 * count : 2 * count + len(slots)], refs[2 * count + len(slots) :]
        for n in range(2 * count):
            value = jnp.dot(sides[n][pl.ds(0, ROWS)], held[n], preferred_element_type=F32)
            if slots and slots[n // 2] == n % 2:
                value = value + carried[n // 2][0, pl.ds(0, ROWS)].astype(F32)
            if whole:
                outs[n][0, pl.ds(0, ROWS)] = value.astype(BF)
                outs[n][0, pl.ds(ROWS, SPARE - ROWS)] = jnp.zeros((SPARE - ROWS, TILE), BF)
                continue
            for h, half in enumerate(halves(value)):
                outs[n // 2 * len(WIDTHS) + h][n % 2] = half.astype(BF)

    shapes = [(1, SPARE, TILE)] * 2 if whole else [(2, ROWS, width) for width in WIDTHS] * count
    flat = pl.pallas_call(
        kernel,
        out_shape=[jax.ShapeDtypeStruct(shape, BF) for shape in shapes],
        in_specs=[VMEM] * (1 + 2 * count + len(slots)),
        out_specs=[VMEM] * len(shapes),
        compiler_params=pltpu.CompilerParams(vmem_limit_bytes=12 << 20),
        cost_estimate=pl.CostEstimate(flops=1 << 10, bytes_accessed=1 << 10, transcendentals=0),
        name="project",
    )(held, *[item for pair in sides for item in pair], *[item for _, item in carry])
    if whole:
        return flat
    return [list(flat[n * len(WIDTHS) : (n + 1) * len(WIDTHS)]) for n in range(count)]


def scale(eigen, parts):
    def kernel(eigen, first, second, third, total, scaled):
        for j in range(2):
            value = first[j].astype(F32) + second[j].astype(F32) + third[j].astype(F32)
            total[j] = value.astype(BF)
            scaled[j] = (value * (1.0 / eigen[j, pl.ds(0, ROWS)])).astype(BF)

    return pl.pallas_call(
        kernel,
        out_shape=[jax.ShapeDtypeStruct(parts[0].shape, BF)] * 2,
        in_specs=[VMEM] * 4,
        out_specs=[VMEM] * 2,
        compiler_params=pltpu.CompilerParams(vmem_limit_bytes=10 << 20),
        cost_estimate=pl.CostEstimate(flops=1 << 10, bytes_accessed=1 << 10, transcendentals=0),
        name="scale",
    )(eigen, *parts)


def places_in(coupled):
    tags = sum(tag_of(own) * (0.5 * 64**d) for d, own in enumerate(coupled[::2]))
    places = jnp.max(tags).astype(jnp.int32)
    return [(places >> (3 * n)) & 7 for n in range(len(coupled))]


def collect(coupled, scaled):
    width, count = scaled[0].shape[2], len(coupled)

    def kernel(*refs):
        coupled, scaled, total = refs[:count], refs[count:-1], refs[-1]
        total[...] = jnp.zeros_like(total)
        for n, place in enumerate(places_in(coupled)):
            total[place] += tdot(coupled[n][pl.ds(0, ROWS)], scaled[n // 2][n % 2])

    return pl.pallas_call(
        kernel,
        out_shape=jax.ShapeDtypeStruct((8, TILE, width), F32),
        in_specs=[VMEM] * (count + len(scaled)),
        out_specs=VMEM,
        compiler_params=pltpu.CompilerParams(vmem_limit_bytes=20 << 20),
        cost_estimate=pl.CostEstimate(flops=1 << 10, bytes_accessed=1 << 10, transcendentals=0),
        name="collect",
    )(*coupled, *scaled)


def correct(total, coupled, scaled):
    width = total.shape[2]

    def kernel(total, *refs):
        coupled, scaled, outs = refs[:2], refs[2:-4], refs[-4:]
        scaled = [ref.at[j] for ref in scaled for j in range(ref.shape[0])]
        places = places_in(coupled)
        terms = [tdot(coupled[j][pl.ds(0, ROWS)], scaled[j][...]) for j in range(2)]
        for k in range(8):
            value = total[k]
            for place, term in zip(places, terms):
                value = value + jnp.where(place == k, term, 0.0)
            outs[k % 4][k // 4] = value.astype(BF)

    return pl.pallas_call(
        kernel,
        out_shape=[jax.ShapeDtypeStruct((2, TILE, width), BF)] * 4,
        in_specs=[VMEM] * (3 + len(scaled)),
        out_specs=[VMEM] * 4,
        compiler_params=pltpu.CompilerParams(vmem_limit_bytes=20 << 20),
        cost_estimate=pl.CostEstimate(flops=1 << 10, bytes_accessed=1 << 10, transcendentals=0),
        name="correct",
    )(total, *coupled, *scaled)


def add(a, b):
    return (a.astype(F32) + b.astype(F32)).astype(BF)


def per_device(stiffness, modes, basis, eigen, counts, ancestry):
    leaf, blk = lax.axis_index("leaf"), lax.axis_index("blk")
    spot = jnp.stack([leaf >> 4, (leaf >> 2) & 3, leaf & 3, blk & 1, counts[0], counts[1], ancestry[0], ancestry[1]])

    crossed = shift(basis, xl=1)
    above, below = shift(basis, y=-1), shift(basis, y=1)
    away = couple(1, spot, modes, stiffness)
    came = [shift(piece, c=1) for piece in away]
    late, crossed = lax.optimization_barrier((spot, crossed))
    kept = couple(0, late, modes, stiffness)
    both = [add(*pair) for pair in zip(kept, came)]
    crossed, _ = lax.optimization_barrier((crossed, both[0]))
    cabove, cbelow = shift(crossed, y=-1), shift(crossed, y=1)
    met2, met13, met0 = (shift(item, xh=1) for item in (both[0], jnp.concatenate(both[1:3]), both[3]))
    met2, above, below = lax.optimization_barrier((met2, above, below))
    own, other = {}, {}
    own[2] = shift(add(both[0][0], met2[0]), z=2)
    mid = TILE // 2
    far1 = shift(jnp.stack([above[:mid], cabove[:mid]]), y=-1)
    far2 = shift(jnp.stack([below[mid:], cbelow[mid:]]), y=1)
    other[2] = shift(own[2][:ROWS], c=1)
    met13, other[2], far1, far2 = lax.optimization_barrier((met13, other[2], far1, far2))
    own[1] = shift(add(both[1][0], met13[0]), z=1)
    own[3] = shift(add(both[2][0], met13[1]), z=3)
    far = jnp.concatenate([far1, far2], axis=1)
    tiles = [basis, above, far[0], below, crossed, cabove, far[1], cbelow]
    part = project([(own[2], other[2])], pick([own[2]], tiles), whole=True)
    carry1, carry3 = shift(part[0], z=-1), shift(part[1], z=1)
    own[1], own[3], met0, _ = lax.optimization_barrier((own[1], own[3], met0, part[0]))
    own[0] = add(both[3][0], met0[0])
    for d in (1, 3, 0):
        other[d] = shift(own[d][:ROWS], c=1)
    held = pick([own[1], own[3]], tiles)
    part1, part3 = project([(own[1], other[1]), (own[3], other[3])], held, [(0, carry1), (1, carry3)])
    (part0,) = project([(own[0], other[0])], pick([own[0]], tiles))
    swap = (blk & 1) == 1
    lam = jnp.where(swap, eigen[::-1], eigen)[:, :, None]
    coupled = [item for d in (0, 1, 3) for item in (own[d], other[d])]
    columns = []
    sums = []
    heard = shift(part1[0], z=-1), shift(part3[0], z=1)
    for h in range(2):
        mine, piece = scale(lam, [part0[h], *heard])
        sums.append(mine)
        up, down = shift(piece, z=1), shift(piece, z=-1)
        far = [shift(up[:1], z=1), shift(down[1:], z=-1)]
        if h == 0:
            part1[1], part3[1], _ = lax.optimization_barrier((part1[1], part3[1], up))
            heard = shift(part1[1], z=-1), shift(part3[1], z=1)
        else:
            mine = jnp.concatenate(sums, axis=2)
            mine = jnp.where(swap, mine[::-1], mine)
            projection = jnp.pad(mine, ((0, 0), (0, 512 - ROWS), (0, 0)))
            far[0], projection = lax.optimization_barrier((far[0], projection))
            piece, ahead, behind = lax.optimization_barrier((piece, ahead, behind))
        terms = correct(collect(coupled, [piece, up, down]), [own[2], other[2]], far)
        if h == 1:
            *terms, total = lax.optimization_barrier((*terms, total))
            columns.append(total)
        ahead, behind = shift(terms[2][:1], y=1), shift(terms[2][1:], y=-1)
        ahead, behind, *_ = lax.optimization_barrier((ahead, behind, *heard))
        ahead = jnp.concatenate([add(terms[1][:1], ahead), terms[1][1:]])
        behind = jnp.concatenate([terms[3][:1], add(terms[3][1:], behind)])
        total = terms[0].astype(F32) + shift(ahead, y=1).astype(F32) + shift(behind, y=-1).astype(F32)
    columns.append(total)
    columns = [total[0] + shift(total[1].astype(BF), xl=1).astype(F32) for total in columns]
    return projection, jnp.concatenate(columns, axis=1)


def solution(mesh):
    placed = (
        P("leaf", "blk", None),
        P("leaf", "blk", None),
        P("leaf", "blk"),
        P("leaf", None),
        P("leaf"),
        P("leaf"),
    )
    return jax.shard_map(
        per_device,
        mesh=mesh,
        in_specs=placed,
        out_specs=(P("leaf", None, "blk"), P("leaf", "blk")),
        check_vma=False,
    )
```
